128 devices in a mesh: seq: 8 (over y, core), mem: 16 (over x, z).
Axes of the slice: x: 4, y: 4, z: 4, core: 2. Of those that a mesh axis runs over, the one named last changes fastest.
Arguments:
- tokens: bfloat16 [16, 2048, 2048], P('mem', 'seq')
- block_ids: int32 [16, 16, 8], P('mem', 'seq'), may hold values from 0 to 127, as said below
- memory: bfloat16 [128, 2, 128, 1024], P('mem')
- w_query: bfloat16 [2048, 1024], replicated, may hold values from -0.125 to 0.125
- w_key: bfloat16 [2048, 1024], replicated, may hold values from -0.125 to 0.125
- w_value: bfloat16 [2048, 1024], replicated, may hold values from -0.125 to 0.125
- w_out: bfloat16 [1024, 2048], replicated, may hold values from -0.1875 to 0.1875
- gate_bias: float32 [8], replicated, may hold values from -2 to 2
Outputs:
- layer_out: bfloat16 [16, 2048, 2048], P('mem', 'seq')
The draws below stay inside these ranges and needn't reach their ends.
Inputs may be any that keep to these rules, and one draw needn't show every extreme that they name: `block_ids`: among the 16 ids of one device (its 2 query blocks), at most 2 are held by the same index m of mem (ids 8m to 8m+7), and some index holds exactly 2; the 8 ids of one query block are distinct.
All inputs are finite; a program needn't handle non-finite values.
Results may differ from the reference program's by a relative error of at most 0.008.
The reference program's roundings to bfloat16 on the way (of `query` and `mixed`) count: a program that leaves them out, or rounds other values in their place, can miss the bound.
Values may be sent and summed in bfloat16 or wider, within the bound.
No kernel may reach another device: no remote copies, remote signals or barrier semaphores. Data moves between devices by JAX's collectives and lax.ppermute only.
A program may use at most 192 MiB of HBM per device.

```python
import jax
import jax.numpy as jnp
from jax import lax

D = 2048
HEADS = 8
HDIM = 128
QBLK = 128
MEMB = 128
TOPB = 8
WIN = 1024
MBLK_DEV = 8
HW = 1024
SEQLEN = 2048
QB_DEV = 2
RQ = 16
CAP = 2
MEM_BLOCKS = 128
N_SEQ = 8
N_MEM = 16


def draw_tokens(key, part):
    key = jax.random.fold_in(key, 5)
    first = jax.random.fold_in(key, 0)
    values = jnp.clip(jax.random.normal(first, (N_MEM, SEQLEN, D), jnp.float32), -6.0, 6.0)
    return values.astype(jnp.bfloat16)


def draw_memory(key, part):
    key = jax.random.fold_in(key, 7)
    first = jax.random.fold_in(key, 0)
    shape = (MEM_BLOCKS, 2, MEMB, HW)
    values = jnp.clip(jax.random.normal(first, shape, jnp.float32), -6.0, 6.0)
    return values.astype(jnp.bfloat16)


def draw_block_ids(key, part):
    key = jax.random.fold_in(key, 11)

    def one_device(subkey):
        key_star, key_other, key_base, key_order = jax.random.split(subkey, 4)
        star = jax.random.randint(key_star, (), 0, N_MEM)
        others = jax.random.permutation(key_other, (N_MEM - 1) * CAP)
        holder = jnp.concatenate([jnp.full((CAP,), star, jnp.int32), ((star + 1 + others % (N_MEM - 1)) % N_MEM).astype(jnp.int32)])[:RQ]
        copies = jnp.concatenate([jnp.arange(CAP, dtype=jnp.int32), (others // (N_MEM - 1)).astype(jnp.int32)])[:RQ]
        base = jax.random.randint(key_base, (N_MEM,), 0, MBLK_DEV)
        local = (base[holder] + copies * (MBLK_DEV // CAP)) % MBLK_DEV
        ids = holder * MBLK_DEV + local
        order = jax.random.permutation(key_order, RQ)
        return ids[order].reshape(QB_DEV, TOPB).astype(jnp.int32)
    subkeys = jax.random.split(key, N_MEM * N_SEQ)
    drawn = jax.vmap(one_device)(subkeys)
    return drawn.reshape(N_MEM, N_SEQ * QB_DEV, TOPB)


def centred(key, extent, spread, reach, kind=jnp.bfloat16):
    return jnp.clip(spread * jax.random.normal(key, extent, jnp.float32), -reach, reach).astype(kind)


def setup_inputs(seed: int = 0) -> dict:
    key_of = jax.random.split(jax.random.key(seed), 9)
    tokens = draw_tokens(jax.random.fold_in(key_of[8], 71), 0)
    block_ids = draw_block_ids(jax.random.fold_in(key_of[8], 71), 0)
    memory = draw_memory(jax.random.fold_in(key_of[8], 71), 0)
    w_query = centred(key_of[3], (D, HW), D ** -0.5, 0.125)
    w_key = centred(key_of[4], (D, HW), D ** -0.5, 0.125)
    w_value = centred(key_of[5], (D, HW), D ** -0.5, 0.125)
    w_out = centred(key_of[6], (HW, D), HW ** -0.5, 0.1875)
    gate_bias = jnp.clip(jax.random.uniform(key_of[7], (HEADS,), jnp.float32, -2.0, 2.0), -2.0, 2.0)
    return {"tokens": tokens, "block_ids": block_ids, "memory": memory, "w_query": w_query, "w_key": w_key, "w_value": w_value, "w_out": w_out, "gate_bias": gate_bias}


def reference(tokens, block_ids, memory, w_query, w_key, w_value, w_out, gate_bias):
    flat = tokens.reshape(N_MEM * SEQLEN, D)

    def project(weight):
        full = jnp.dot(flat, weight, preferred_element_type=jnp.float32).astype(jnp.bfloat16)
        return full.reshape(N_MEM, SEQLEN, HEADS, HDIM)

    query = project(w_query)
    keys = project(w_key)
    values = project(w_value)
    scale = HDIM ** -0.5
    blocks = SEQLEN // QBLK
    padding = jnp.zeros((N_MEM, WIN, HEADS, HDIM), jnp.bfloat16)
    keys_pad = jnp.concatenate([padding, keys], axis=1)
    values_pad = jnp.concatenate([padding, values], axis=1)
    zero = jnp.zeros((), jnp.int32)

    def local_block(index):
        sequence = (index // blocks).astype(jnp.int32)
        start = ((index % blocks) * QBLK).astype(jnp.int32)
        qpart = lax.dynamic_slice(query, (sequence, start, zero, zero), (1, QBLK, HEADS, HDIM))[0].astype(jnp.float32)
        kpart = lax.dynamic_slice(keys_pad, (sequence, start, zero, zero), (1, WIN + QBLK, HEADS, HDIM))[0].astype(jnp.float32)
        vpart = lax.dynamic_slice(values_pad, (sequence, start, zero, zero), (1, WIN + QBLK, HEADS, HDIM))[0].astype(jnp.float32)
        scores = jnp.einsum("qhd,khd->hqk", qpart, kpart) * scale
        qpos = start + jnp.arange(QBLK, dtype=jnp.int32)
        kpos = start - WIN + jnp.arange(WIN + QBLK, dtype=jnp.int32)
        valid = (kpos[None, :] >= 0) & (kpos[None, :] <= qpos[:, None]) & (qpos[:, None] - kpos[None, :] < WIN)
        scores = jnp.where(valid[None], scores, -1e30)
        probs = jax.nn.softmax(scores, axis=-1).astype(jnp.bfloat16)
        return jnp.einsum("hqk,khd->qhd", probs.astype(jnp.float32), vpart)

    local_out = lax.map(local_block, jnp.arange(N_MEM * blocks, dtype=jnp.int32))

    query_blocks = query.reshape(N_MEM * blocks, QBLK, HEADS, HDIM)
    flat_ids = block_ids.reshape(N_MEM * blocks, TOPB)

    def memory_block(pair):
        qpart, ids = pair
        tiles = memory[ids]
        kpart = tiles[:, 0].reshape(TOPB * MEMB, HEADS, HDIM).astype(jnp.float32)
        vpart = tiles[:, 1].reshape(TOPB * MEMB, HEADS, HDIM).astype(jnp.float32)
        scores = jnp.einsum("qhd,khd->hqk", qpart.astype(jnp.float32), kpart) * scale
        probs = jax.nn.softmax(scores, axis=-1).astype(jnp.bfloat16)
        return jnp.einsum("hqk,khd->qhd", probs.astype(jnp.float32), vpart)

    memory_out = lax.map(memory_block, (query_blocks, flat_ids))
    gate = jax.nn.sigmoid(gate_bias)[:, None]
    mixed = (gate * memory_out + (1.0 - gate) * local_out).astype(jnp.bfloat16)
    mixed = mixed.reshape(N_MEM * SEQLEN, HW)
    result = jnp.dot(mixed, w_out, preferred_element_type=jnp.float32).astype(jnp.bfloat16)
    return result.reshape(N_MEM, SEQLEN, D)
```

```python
import functools

import jax
import jax.numpy as jnp
from jax import lax
from jax.experimental import pallas as pl
from jax.experimental.pallas import tpu as pltpu
from jax.sharding import PartitionSpec as P

RING = 4
HD = 128
FEAT = 512
TOK = 256
CHIP = 512
BLK = 128
STAT = 16
SLAB = FEAT + STAT
NEG = -1e30
F32 = jnp.float32
BF16 = jnp.bfloat16
LOG2E = 1.4426950408889634
VMEM = 48 * 1024 * 1024


def index_of(x, y, z, c):
    return (y * 2 + c) * RING * RING + x * RING + z


def send(array, move):
    pairs = []
    for x in range(RING):
        for z in range(RING):
            for y in range(RING):
                for c in range(2):
                    to = move(x, y, z, c)
                    if to is not None:
                        pairs.append((index_of(x, y, z, c), index_of(*to)))
    return lax.ppermute(array, ("seq", "mem"), pairs)


def step(c):
    return 1 if c == 0 else -1


def x1(x, y, z, c):
    return ((x + step(c)) % RING, y, z, c)


def x2(x, y, z, c):
    return ((x - step(c)) % RING, y, z, c)


def z1(x, y, z, c):
    return (x, y, (z + step(c)) % RING, c)


def z2(x, y, z, c):
    return (x, y, (z - step(c)) % RING, c)


def y1(x, y, z, c):
    return (x, (y + step(c)) % RING, z, c)


def y2(x, y, z, c):
    return (x, (y - step(c)) % RING, z, c)


def yfar(x, y, z, c):
    return (x, (y + 2) % RING, z, c)


def later1(x, y, z, c):
    return (x, y + 1, z, c) if y + 1 < RING else None


def later2(x, y, z, c):
    return (x, y + 2, z, c) if y + 2 < RING else None


def core(x, y, z, c):
    return (x, y, z, 1 - c)


def params():
    return pltpu.CompilerParams(vmem_limit_bytes=VMEM)


def cost(flops, nbytes, trans=0):
    return pl.CostEstimate(flops=flops, bytes_accessed=nbytes, transcendentals=trans)


def any_specs(count):
    return [pl.BlockSpec(memory_space=pl.ANY)] * count


def dot(a, b, ca, cb):
    return lax.dot_general(a, b, (((ca,), (cb,)), ((), ())), preferred_element_type=F32)


def query_kernel(info, own, oth, w, ids, out):
    out[0:TOK, :] = dot(own[...], w[...], 1, 0).astype(BF16)
    out[TOK:CHIP, :] = dot(oth[...], w[...], 1, 0).astype(BF16)
    out[CHIP:, :] = ids[...]


def project_query(info, own, oth, w, ids):
    depth = own.shape[1]
    tile = 256
    steps = FEAT // tile
    whole = pl.BlockSpec((TOK, depth), lambda j, info: (0, 0))
    return pl.pallas_call(
        query_kernel,
        grid_spec=pltpu.PrefetchScalarGridSpec(
            num_scalar_prefetch=1,
            grid=(steps,),
            in_specs=[
                whole,
                whole,
                pl.BlockSpec((depth, tile), lambda j, info: (0, info[3] * steps + j)),
                pl.BlockSpec((STAT, tile), lambda j, info: (0, j)),
            ],
            out_specs=pl.BlockSpec((CHIP + STAT, tile), lambda j, info: (0, j)),
        ),
        out_shape=jax.ShapeDtypeStruct((CHIP + STAT, FEAT), BF16),
        compiler_params=params(),
        cost_estimate=cost(2 * CHIP * depth * FEAT, 2 * depth * (FEAT + CHIP)),
    )(info, own, oth, w, ids)


def keyvalue_kernel(info, own, oth, wk, wv, k, v):
    for w, out in ((wk, k), (wv, v)):
        out[0:TOK, :] = dot(own[...], w[...], 1, 0).astype(BF16)
        out[TOK:CHIP, :] = dot(oth[...], w[...], 1, 0).astype(BF16)


def project_keyvalue(info, own, oth, wk, wv):
    depth = own.shape[1]
    tile = 256
    steps = FEAT // tile
    whole = pl.BlockSpec((TOK, depth), lambda j, info: (0, 0))
    weight = pl.BlockSpec((depth, tile), lambda j, info: (0, info[3] * steps + j))
    result = pl.BlockSpec((CHIP, tile), lambda j, info: (0, j))
    return pl.pallas_call(
        keyvalue_kernel,
        grid_spec=pltpu.PrefetchScalarGridSpec(
            num_scalar_prefetch=1,
            grid=(steps,),
            in_specs=[whole, whole, weight, weight],
            out_specs=[result, result],
        ),
        out_shape=[jax.ShapeDtypeStruct((CHIP, FEAT), BF16)] * 2,
        compiler_params=params(),
        cost_estimate=cost(4 * CHIP * depth * FEAT, 2 * depth * (2 * FEAT + CHIP)),
    )(info, own, oth, wk, wv)


def split3(value):
    high = value.astype(BF16).astype(F32)
    rest = value - high
    mid = rest.astype(BF16).astype(F32)
    return high, mid, rest - mid


def pack_stats(values, width):
    row = lax.broadcasted_iota(jnp.int32, (STAT, width), 0)
    packed = jnp.zeros((STAT, width), F32)
    for h, value in enumerate(values):
        for i, part in enumerate(split3(value)):
            packed = jnp.where(row == 3 * h + i, part, packed)
    return packed.astype(BF16)


def local_kernel(info, qa, q1, q2, q3, k_hbm, v_hbm, o0, o1, o2, q, k, v, o, sem, osem):
    y = info[1]
    c = info[3]
    rows = pl.ds(0, CHIP)
    copies = [
        pltpu.make_async_copy(k_hbm, k, sem.at[0]),
        pltpu.make_async_copy(v_hbm, v, sem.at[1]),
        pltpu.make_async_copy(qa.at[rows], q.at[0], sem.at[2]),
        pltpu.make_async_copy(q3.at[rows], q.at[2], sem.at[3]),
    ]
    for copy in copies:
        copy.start()

    @pl.when(c == 0)
    def _():
        pltpu.make_async_copy(q2.at[rows], q.at[1], sem.at[4]).start()

    @pl.when(c != 0)
    def _():
        pltpu.make_async_copy(q1.at[rows], q.at[1], sem.at[4]).start()

    for copy in copies:
        copy.wait()
    pltpu.make_async_copy(q2.at[rows], q.at[1], sem.at[4]).wait()

    factor = HD ** -0.5 * LOG2E
    j = lax.broadcasted_iota(jnp.int32, (CHIP, TOK), 0)
    i = lax.broadcasted_iota(jnp.int32, (CHIP, TOK), 1)
    kpos = jnp.where(j < TOK, j + c * TOK, j - TOK + (1 - c) * TOK)

    def unit(t, carry):
        d = t // 2
        half = t % 2

        @pl.when(y + d < RING)
        def _():
            place = jnp.where(half == 0, c, 1 - c) * TOK
            diff = i - kpos + (place + d * CHIP)
            valid = (diff >= 0) & (diff < 2 * CHIP)
            start = pl.multiple_of(half * TOK, TOK)
            stats = []
            for h in range(FEAT // HD):
                cols = slice(h * HD, (h + 1) * HD)
                s = dot(k[:, cols], q[d, pl.ds(start, TOK), cols], 1, 1) * factor
                s = jnp.where(valid, s, NEG)
                m = jnp.max(s, axis=0, keepdims=True)
                p = jnp.exp2(s - m)
                total = jnp.sum(p, axis=0, keepdims=True)
                out = dot(v[:, cols], p.astype(BF16), 0, 0) / total
                o[d, cols, pl.ds(start, TOK)] = out.astype(BF16)
                stats.append(m + jnp.log2(total))
            o[d, FEAT:, pl.ds(start, TOK)] = pack_stats(stats, TOK)

        return carry

    lax.fori_loop(0, 6, unit, 0)
    outs = [
        pltpu.make_async_copy(o.at[d], ref, osem.at[d])
        for d, ref in enumerate((o0, o1, o2))
    ]
    for copy in outs:
        copy.start()
    for copy in outs:
        copy.wait()


def local_attention(info, queries, k, v):
    slab = jax.ShapeDtypeStruct((SLAB, CHIP), BF16)
    return pl.pallas_call(
        local_kernel,
        grid_spec=pltpu.PrefetchScalarGridSpec(
            num_scalar_prefetch=1,
            grid=(1,),
            in_specs=any_specs(6),
            out_specs=any_specs(3),
            scratch_shapes=[
                pltpu.VMEM((3, CHIP, FEAT), BF16),
                pltpu.VMEM((CHIP, FEAT), BF16),
                pltpu.VMEM((CHIP, FEAT), BF16),
                pltpu.VMEM((3, SLAB, CHIP), BF16),
                pltpu.SemaphoreType.DMA((5,)),
                pltpu.SemaphoreType.DMA((3,)),
            ],
        ),
        out_shape=[slab] * 3,
        compiler_params=params(),
        cost_estimate=cost(12 * CHIP * CHIP * FEAT, 8 * 2 * CHIP * FEAT, 12 * CHIP * CHIP),
    )(info, *queries, k, v)


def memory_kernel(info, ids, *refs):
    queries, parts_a, parts_b, outs = refs[:4], refs[4:8], refs[8:12], refs[12:16]
    q, mem, o, slots, sem, osem = refs[16:]
    x, y, z, c = info[0], info[1], info[2], info[3]
    copies = [
        pltpu.make_async_copy(ref.at[pl.ds(0, CHIP)], q.at[s], sem.at[s])
        for s, ref in enumerate(queries)
    ]
    for s in range(RING):
        for first, parts in ((0, parts_a), (16, parts_b)):
            copies.append(
                pltpu.make_async_copy(
                    parts[s],
                    mem.at[pl.ds(first + 4 * s, 4)],
                    sem.at[4 + s + first // 4],
                )
            )
    for copy in copies:
        copy.start()
    for copy in copies:
        copy.wait()

    factor = HD ** -0.5 * LOG2E

    def arrival(relative):
        near = jnp.where((relative == 3) == (c == 0), 1, 2)
        return jnp.where(relative == 0, 0, jnp.where(relative == 2, 3, near))

    def block(n, carry):
        s = n // 4
        start = pl.multiple_of((n % 4) * BLK, BLK)

        def look(t, count):
            ident = ids[n * 8 + t]
            mine = ((ident >> 1) & 3) == y
            ax = arrival(((ident >> 5) - x) & 3)
            az = arrival((((ident >> 3) & 3) - z) & 3)
            slot = jnp.where((ident & 1) == 0, az * 4 + ax, 16 + ax * 4 + az)
            slots[count] = slot
            return count + mine.astype(jnp.int32)

        for t in range(8):
            slots[t] = 0
        count = lax.fori_loop(0, 8, look, 0)
        pairs = (count + 1) // 2

        @pl.when(pairs == 0)
        def _():
            o[s, 0:FEAT, pl.ds(start, BLK)] = jnp.zeros((FEAT, BLK), BF16)
            low = jnp.full((1, BLK), NEG, F32)
            o[s, FEAT:, pl.ds(start, BLK)] = pack_stats([low] * (FEAT // HD), BLK)

        def attend(size):
            chosen = [slots[t] for t in range(size)]
            stats = []
            for h in range(FEAT // HD):
                cols = slice(h * HD, (h + 1) * HD)
                qh = q[s, pl.ds(start, BLK), cols]
                scores = [dot(mem[t, 0, :, cols], qh, 1, 1) * factor for t in chosen]
                scores[-1] = jnp.where(count == size, scores[-1], NEG)
                m = functools.reduce(jnp.maximum, scores)
                m = jnp.max(m, axis=0, keepdims=True)
                probs = [jnp.exp2(score - m) for score in scores]
                total = jnp.sum(functools.reduce(jnp.add, probs), axis=0, keepdims=True)
                out = functools.reduce(
                    jnp.add,
                    [
                        dot(mem[t, 1, :, cols], p.astype(BF16), 0, 0)
                        for t, p in zip(chosen, probs)
                    ],
                )
                o[s, cols, pl.ds(start, BLK)] = (out / total).astype(BF16)
                stats.append(m + jnp.log2(total))
            o[s, FEAT:, pl.ds(start, BLK)] = pack_stats(stats, BLK)

        for size in range(1, 5):
            pl.when(pairs == size)(functools.partial(attend, 2 * size))
        return carry

    lax.fori_loop(0, 16, block, 0)
    backs = [
        pltpu.make_async_copy(o.at[s], ref, osem.at[s]) for s, ref in enumerate(outs)
    ]
    for copy in backs:
        copy.start()
    for copy in backs:
        copy.wait()


def memory_attention(info, ids, queries, parts_a, parts_b):
    slab = jax.ShapeDtypeStruct((SLAB, CHIP), BF16)
    return pl.pallas_call(
        memory_kernel,
        grid_spec=pltpu.PrefetchScalarGridSpec(
            num_scalar_prefetch=2,
            grid=(1,),
            in_specs=any_specs(12),
            out_specs=any_specs(4),
            scratch_shapes=[
                pltpu.VMEM((4, CHIP, FEAT), BF16),
                pltpu.VMEM((32, 2, BLK, FEAT), BF16),
                pltpu.VMEM((4, SLAB, CHIP), BF16),
                pltpu.SMEM((16,), jnp.int32),
                pltpu.SemaphoreType.DMA((12,)),
                pltpu.SemaphoreType.DMA((4,)),
            ],
        ),
        out_shape=[slab] * 4,
        compiler_params=params(),
        cost_estimate=cost(32 * 4 * BLK * BLK * FEAT, 12 * 2**20, 32 * 4 * BLK * BLK),
    )(info, ids, *queries, *parts_a, *parts_b)


def merge_kernel(info, gate, m0, m1, m2, m3, l0, l1, l2, own, oth):
    y = info[1]
    heads = FEAT // HD

    def merged(refs, shown, h, share):
        logs = []
        for ref, show in zip(refs, shown):
            rows = ref[FEAT:, :].astype(F32)
            log = rows[3 * h : 3 * h + 1] + rows[3 * h + 1 : 3 * h + 2]
            log = log + rows[3 * h + 2 : 3 * h + 3]
            logs.append(log if show is None else jnp.where(show, log, NEG))
        top = functools.reduce(jnp.maximum, logs)
        weights = [jnp.exp2(log - top) for log in logs]
        scale = share / functools.reduce(jnp.add, weights)
        total = None
        for ref, weight in zip(refs, weights):
            term = ref[h * HD : (h + 1) * HD, :].astype(F32) * (weight * scale)
            total = term if total is None else total + term
        return total

    for h in range(heads):
        g = jax.nn.sigmoid(jnp.full((1, CHIP), gate[info[3] * heads + h], F32))
        mix = merged((m0, m1, m2, m3), (None,) * 4, h, g)
        mix = mix + merged((l0, l1, l2), (None, y >= 1, y >= 2), h, 1.0 - g)
        mix = mix.astype(BF16)
        own[h * HD : (h + 1) * HD, :] = mix[:, :TOK]
        oth[h * HD : (h + 1) * HD, :] = mix[:, TOK:]


def merge(info, gate, slabs):
    whole = pl.BlockSpec((SLAB, CHIP), lambda j, info, gate: (0, 0))
    half = pl.BlockSpec((FEAT, TOK), lambda j, info, gate: (0, 0))
    return pl.pallas_call(
        merge_kernel,
        grid_spec=pltpu.PrefetchScalarGridSpec(
            num_scalar_prefetch=2,
            grid=(1,),
            in_specs=[whole] * 7,
            out_specs=[half] * 2,
        ),
        out_shape=[jax.ShapeDtypeStruct((FEAT, TOK), BF16)] * 2,
        compiler_params=params(),
        cost_estimate=cost(20 * SLAB * CHIP, 8 * 2 * SLAB * CHIP),
    )(info, gate, *slabs)


def output_kernel(info, own, oth, w_own, w_oth, out):
    total = dot(own[...], w_own[...], 0, 0) + dot(oth[...], w_oth[...], 0, 0)
    out[...] = total.astype(BF16)


def project_output(info, own, oth, w):
    width = w.shape[1]
    tile = 512
    half = pl.BlockSpec((FEAT, TOK), lambda j, info: (0, 0))
    return pl.pallas_call(
        output_kernel,
        grid_spec=pltpu.PrefetchScalarGridSpec(
            num_scalar_prefetch=1,
            grid=(width // tile,),
            in_specs=[
                half,
                half,
                pl.BlockSpec((FEAT, tile), lambda j, info: (info[3], j)),
                pl.BlockSpec((FEAT, tile), lambda j, info: (1 - info[3], j)),
            ],
            out_specs=pl.BlockSpec((TOK, tile), lambda j, info: (0, j)),
        ),
        out_shape=jax.ShapeDtypeStruct((TOK, width), BF16),
        compiler_params=params(),
        cost_estimate=cost(4 * TOK * FEAT * width, 4 * FEAT * width),
    )(info, own, oth, w, w)


def ring(array, first, second):
    near = send(array, first)
    other = send(array, second)
    return [array, near, other, send(near, first)]


def shards(tokens, block_ids, memory, w_query, w_key, w_value, w_out, gate_bias):
    mem = lax.axis_index("mem")
    seq = lax.axis_index("seq")
    y, c = seq // 2, seq % 2
    info = jnp.stack([mem // RING, y, mem % RING, c]).astype(jnp.int32)

    part = lax.dynamic_slice(memory, (2 * y, 0, 0, c * FEAT), (2, 2, BLK, FEAT))
    gathered_a = jnp.concatenate(ring(part[0:1], x1, x2))
    gathered_b = jnp.concatenate(ring(part[1:2], z1, z2))
    parts_a = ring(gathered_a, z1, z2)
    parts_b = ring(gathered_b, x1, x2)

    own = tokens[0]
    oth = send(own, core)
    ids_own = block_ids.reshape(1, 16)
    ids_chip = jnp.concatenate([ids_own, send(ids_own, core)], axis=1)
    ids_rows = jnp.zeros((STAT, FEAT), BF16).at[0:1, 0:32].set(ids_chip.astype(BF16))
    query = project_query(info, own, oth, w_query, ids_rows)
    queries = ring(query, y1, y2)
    k, v = project_keyvalue(info, own, oth, w_key, w_value)
    ids = jnp.concatenate([q[CHIP, 0:32] for q in queries]).astype(jnp.int32)

    local0, local1, local2 = local_attention(info, queries, k, v)
    local1 = send(local1, later1)
    local2 = send(local2, later2)

    part0, part1, part2, part3 = memory_attention(info, ids, queries, parts_a, parts_b)
    slabs = [part0, send(part1, y2), send(part2, y1), send(part3, yfar)]
    mix_own, mix_oth = merge(info, gate_bias, slabs + [local0, local1, local2])
    mix_oth = send(mix_oth, core)
    return project_output(info, mix_own, mix_oth, w_out)[None]


def solution(mesh):
    in_specs = (
        P("mem", "seq", None),
        P("mem", "seq", None),
        P("mem", None, None, None),
        P(),
        P(),
        P(),
        P(),
        P(),
    )
    out_specs = P("mem", "seq", None)
    return jax.shard_map(shards, mesh=mesh, in_specs=in_specs, out_specs=out_specs, check_vma=False)
```

```python
import functools

import jax
import jax.numpy as jnp
from jax import lax
from jax.experimental import pallas as pl
from jax.experimental.pallas import tpu as pltpu
from jax.sharding import PartitionSpec as P

RING = 4
HD = 128
FEAT = 512
HEADS = FEAT // HD
GROUP = 2
UNROLL = 4
TOK = 256
CHIP = 512
BLK = 128
STAT = 16
SLAB = FEAT + STAT
NEG = -1e30
F32 = jnp.float32
BF16 = jnp.bfloat16
LOG2E = 1.4426950408889634
VMEM = 24 * 1024 * 1024
WIDE_VMEM = 60 * 1024 * 1024


def index_of(x, y, z, c):
    return (y * 2 + c) * RING * RING + x * RING + z


def send(array, move):
    pairs = []
    for x in range(RING):
        for z in range(RING):
            for y in range(RING):
                for c in range(2):
                    to = move(x, y, z, c)
                    if to is not None:
                        pairs.append((index_of(x, y, z, c), index_of(*to)))
    return lax.ppermute(array, ("seq", "mem"), pairs)


def gather_move(phase, distance):
    def move(x, y, z, c):
        if (phase == 0) == (c == 0):
            return ((x + distance) % RING, y, z, c)
        return (x, y, (z + distance) % RING, c)

    return move


def around(distance):
    def move(x, y, z, c):
        return (x, (y + (distance if c == 0 else -distance)) % RING, z, c)

    return move


def later1(x, y, z, c):
    return (x, y + 1, z, c) if y + 1 < RING else None


def later2(x, y, z, c):
    return (x, y + 2, z, c) if y + 2 < RING else None


def core(x, y, z, c):
    return (x, y, z, 1 - c)


def params(limit=VMEM):
    return pltpu.CompilerParams(vmem_limit_bytes=limit)


def after(value, *earlier):
    return lax.optimization_barrier((value, earlier))[0]


def cost(flops, nbytes, trans=0):
    return pl.CostEstimate(flops=flops, bytes_accessed=nbytes, transcendentals=trans)


def any_specs(count):
    return [pl.BlockSpec(memory_space=pl.ANY)] * count


def dot(a, b, ca, cb):
    return lax.dot_general(a, b, (((ca,), (cb,)), ((), ())), preferred_element_type=F32)


def query_kernel(info, own, oth, w, ids, out):
    out[0:TOK, :] = dot(own[...], w[...], 1, 0).astype(BF16)
    out[TOK:CHIP, :] = dot(oth[...], w[...], 1, 0).astype(BF16)
    out[CHIP:, :] = ids[...]


def project_query(info, own, oth, w, ids):
    depth = own.shape[1]
    tile = 256
    steps = FEAT // tile
    whole = pl.BlockSpec((TOK, depth), lambda j, info: (0, 0))
    return pl.pallas_call(
        query_kernel,
        grid_spec=pltpu.PrefetchScalarGridSpec(
            num_scalar_prefetch=1,
            grid=(steps,),
            in_specs=[
                whole,
                whole,
                pl.BlockSpec((depth, tile), lambda j, info: (0, info[3] * steps + j)),
                pl.BlockSpec((STAT, tile), lambda j, info: (0, j)),
            ],
            out_specs=pl.BlockSpec((CHIP + STAT, tile), lambda j, info: (0, j)),
        ),
        out_shape=jax.ShapeDtypeStruct((CHIP + STAT, FEAT), BF16),
        compiler_params=params(WIDE_VMEM),
        cost_estimate=cost(2 * CHIP * depth * FEAT, 2 * depth * (FEAT + CHIP)),
    )(info, own, oth, w, ids)


def keyvalue_kernel(info, own, oth, wk, wv, k, v):
    for tok, place in ((own, slice(0, TOK)), (oth, slice(TOK, CHIP))):
        k[place, :] = dot(tok[...], wk[...], 1, 0).astype(BF16)
        v[:, place] = dot(tok[...], wv[...], 1, 0).astype(BF16).T


def project_keyvalue(info, own, oth, wk, wv):
    depth = own.shape[1]
    tile = 256
    steps = FEAT // tile
    whole = pl.BlockSpec((TOK, depth), lambda j, info: (0, 0))
    weight = pl.BlockSpec((depth, tile), lambda j, info: (0, info[3] * steps + j))
    result = pl.BlockSpec((CHIP, tile), lambda j, info: (0, j))
    return pl.pallas_call(
        keyvalue_kernel,
        grid_spec=pltpu.PrefetchScalarGridSpec(
            num_scalar_prefetch=1,
            grid=(steps,),
            in_specs=[whole, whole, weight, weight],
            out_specs=[result, pl.BlockSpec((tile, CHIP), lambda j, info: (j, 0))],
        ),
        out_shape=[jax.ShapeDtypeStruct((CHIP, FEAT), BF16)] * 2,
        compiler_params=params(WIDE_VMEM),
        cost_estimate=cost(4 * CHIP * depth * FEAT, 2 * depth * (2 * FEAT + CHIP)),
    )(info, own, oth, wk, wv)


def split3(value):
    high = value.astype(BF16).astype(F32)
    rest = value - high
    mid = rest.astype(BF16).astype(F32)
    return high, mid, rest - mid


def pack_stats(values, width):
    row = lax.broadcasted_iota(jnp.int32, (STAT, width), 0)
    packed = jnp.zeros((STAT, width), F32)
    for h, value in enumerate(values):
        for i, part in enumerate(split3(value)):
            packed = jnp.where(row == 3 * h + i, part, packed)
    return packed.astype(BF16)


def local_block(distance, info, q, k, v, out):
    c = info[3]
    factor = HD ** -0.5 * LOG2E
    key = lax.broadcasted_iota(jnp.int32, (TOK, TOK), 0)
    ask = lax.broadcasted_iota(jnp.int32, (TOK, TOK), 1)
    valid = {0: ask >= key, 1: None, 2: ask < key}[distance]

    def half(place, halves):
        rows = slice(place * TOK, (place + 1) * TOK)
        stats = []
        for h in range(HEADS):
            cols = slice(h * HD, (h + 1) * HD)
            scores = []
            for i in halves:
                s = dot(k[i * TOK : (i + 1) * TOK, cols], q[rows, cols], 1, 1) * factor
                if i == place and valid is not None:
                    s = jnp.where(valid, s, NEG)
                scores.append(s)
            m = jnp.max(functools.reduce(jnp.maximum, scores), axis=0, keepdims=True)
            probs = [jnp.exp2(s - m) for s in scores]
            total = jnp.sum(functools.reduce(jnp.add, probs), axis=0, keepdims=True)
            parts = [
                dot(v[cols, i * TOK : (i + 1) * TOK], p.astype(BF16), 1, 0)
                for i, p in zip(halves, probs)
            ]
            mix = functools.reduce(jnp.add, parts)
            out[cols, rows] = (mix * (1.0 / total)).astype(BF16)
            stats.append(m + jnp.log2(total))
        out[FEAT:, rows] = pack_stats(stats, TOK)

    for place in range(2):
        if distance == 1:
            half(place, (0, 1))
            continue
        later = (place + c) == 1
        both = later if distance == 0 else jnp.logical_not(later)
        pl.when(both)(functools.partial(half, place, (0, 1)))
        pl.when(jnp.logical_not(both))(functools.partial(half, place, (place,)))


def same_kernel(info, q, k, v, out):
    local_block(0, info, q, k, v, out)


def next_kernel(info, q1, q2, q3, k, v, out1, out2):
    y, c = info[1], info[3]
    for near, here in ((q2, c == 0), (q1, c != 0)):

        @pl.when((y + 1 < RING) & here)
        def _():
            local_block(1, info, near, k, v, out1)

    @pl.when(y + 2 < RING)
    def _():
        local_block(2, info, q3, k, v, out2)


def local_attention(kernel, info, queries, k, v, count):
    slab = jax.ShapeDtypeStruct((SLAB, CHIP), BF16)

    def whole(array):
        return pl.BlockSpec(array.shape, lambda j, info: (0, 0))

    return pl.pallas_call(
        kernel,
        grid_spec=pltpu.PrefetchScalarGridSpec(
            num_scalar_prefetch=1,
            grid=(1,),
            in_specs=[whole(a) for a in (*queries, k, v)],
            out_specs=[whole(slab)] * count,
        ),
        out_shape=[slab] * count,
        compiler_params=params(),
        cost_estimate=cost(4 * count * CHIP * CHIP * FEAT, 8 * CHIP * FEAT, 4 * CHIP * CHIP),
    )(info, *queries, k, v)


def part_kernel(info, mem, out, held, sem):
    start = pl.multiple_of(info[3] * FEAT, FEAT)
    src = mem.at[pl.ds(2 * info[1], 2), :, :, pl.ds(start, FEAT)]
    copy = pltpu.make_async_copy(src, held, sem)
    copy.start()
    copy.wait()
    for block in range(2):
        for h in range(HEADS):
            cols = slice(h * HD, (h + 1) * HD)
            out[0, h // GROUP, block, 0, h % GROUP] = held[block, 0, :, cols]
            out[0, h // GROUP, block, 1, h % GROUP] = held[block, 1, :, cols].T


def take_part(info, memory):
    shape = (1, HEADS // GROUP, 2, 2, GROUP, BLK, HD)
    return pl.pallas_call(
        part_kernel,
        grid_spec=pltpu.PrefetchScalarGridSpec(
            num_scalar_prefetch=1,
            grid=(1,),
            in_specs=[pl.BlockSpec(memory_space=pltpu.HBM)],
            out_specs=pl.BlockSpec(shape, lambda j, info: (0,) * 7),
            scratch_shapes=[
                pltpu.VMEM((2, 2, BLK, FEAT), BF16),
                pltpu.SemaphoreType.DMA,
            ],
        ),
        out_shape=jax.ShapeDtypeStruct(shape, BF16),
        compiler_params=params(WIDE_VMEM),
        cost_estimate=cost(0, 2**20),
    )(info, memory)


def plan_kernel(info, ids, slots, blocks):
    x, y, z, c = info[0], info[1], info[2], info[3]
    order = 120
    shift_x = jnp.where(c == 0, 0, 2)

    def look(n, used):
        count = used
        for t in range(8):
            ident = ids[n * 8 + t]
            ax = (order >> ((((ident >> 5) - x) & 3) * 2)) & 3
            az = (order >> (((((ident >> 3) & 3) - z) & 3) * 2)) & 3
            slot = (ax << shift_x) + (az << (2 - shift_x))
            slots[count] = slot * 2 + (ident & 1)
            blocks[count >> 1] = n
            count = count + (((ident >> 1) & 3) == y).astype(jnp.int32)
        slots[count] = 32
        return count + (count & 1)

    used = lax.fori_loop(0, 16, look, 0)
    units = used >> 1
    for u in range(UNROLL - 1):
        blocks[units + u] = 16
        slots[used + 2 * u] = 0
        slots[used + 2 * u + 1] = 32
    blocks[79] = (units + UNROLL - 1) // UNROLL


def plan_units(info, ids):
    smem = pl.BlockSpec(memory_space=pltpu.SMEM)
    return pl.pallas_call(
        plan_kernel,
        in_specs=[smem] * 2,
        out_specs=[smem] * 2,
        out_shape=[
            jax.ShapeDtypeStruct((144,), jnp.int32),
            jax.ShapeDtypeStruct((80,), jnp.int32),
        ],
        compiler_params=params(),
        cost_estimate=cost(1000, 1000),
    )(info, ids)


def memory_kernel(group, slots, blocks, *refs):
    queries, parts, outs = refs[:4], refs[4:8], refs[8:12]
    q, mem, acc, top, low, o, sem, osem = refs[12:]
    wide = GROUP * HD
    copies = [
        pltpu.make_async_copy(ref, mem.at[pl.ds(4 * s, 4)], sem.at[4 + s])
        for s, ref in enumerate(parts)
    ]
    for s, ref in enumerate(queries):
        src = ref.at[pl.ds(0, CHIP), pl.ds(group * wide, wide)]
        copies.append(pltpu.make_async_copy(src, q.at[s], sem.at[s]))
    for copy in copies:
        copy.start()

    acc[...] = jnp.zeros_like(acc)
    top[...] = jnp.full_like(top, NEG)
    low[...] = jnp.zeros_like(low)
    for copy in copies:
        copy.wait()

    factor = HD ** -0.5 * LOG2E

    def pair(i, carry):
        work = []
        for u in [UNROLL * i + k for k in range(UNROLL)]:
            n = blocks[u]
            from_q = jnp.minimum(n, 15)
            start = pl.multiple_of((from_q & 3) * BLK, BLK)
            second = slots[2 * u + 1]
            work.append((n, from_q >> 2, start, slots[2 * u], second & 31, second < 32))
        scores = {}
        for j, (n, s, start, one, two, full) in enumerate(work):
            for h in range(GROUP):
                keys = jnp.concatenate([mem[one >> 1, one & 1, 0, h], mem[two >> 1, two & 1, 0, h]], axis=0)
                qh = q[s, pl.ds(start, BLK), h * HD : (h + 1) * HD]
                scores[j, h] = dot(keys, qh, 1, 1) * factor
        for j, (n, s, start, one, two, full) in enumerate(work):
            for h in range(GROUP):
                first, last = scores[j, h][:BLK], scores[j, h][BLK:]
                last = jnp.where(full, last, NEG)
                m_old = top[n, h]
                m = jnp.max(jnp.maximum(first, last), axis=0, keepdims=True)
                m = jnp.maximum(m_old, m)
                p = jnp.concatenate([jnp.exp2(first - m), jnp.exp2(last - m)], axis=0)
                alpha = jnp.exp2(m_old - m)
                top[n, h] = m
                low[n, h] = low[n, h] * alpha + jnp.sum(p, axis=0, keepdims=True)
                values = jnp.concatenate([mem[one >> 1, one & 1, 1, h], mem[two >> 1, two & 1, 1, h]], axis=1)
                acc[n, h] = acc[n, h] * alpha + dot(values, p.astype(BF16), 1, 0)
        return carry

    lax.fori_loop(0, blocks[79], pair, 0)

    backs = [
        pltpu.make_async_copy(o.at[s], ref, osem.at[s]) for s, ref in enumerate(outs)
    ]
    for s in (3, 1, 2, 0):
        for b in range(4):
            n = s * 4 + b
            cols = slice(b * BLK, (b + 1) * BLK)
            stats = []
            for h in range(GROUP):
                total = low[n, h]
                some = total > 0.0
                total = jnp.where(some, total, 1.0)
                o[s, h * HD : (h + 1) * HD, cols] = (acc[n, h] * (1.0 / total)).astype(BF16)
                stats.append(jnp.where(some, top[n, h] + jnp.log2(total), NEG))
            o[s, wide:, cols] = pack_stats(stats, BLK)
        backs[s].start()
    for copy in backs:
        copy.wait()


def memory_attention(group, plan, queries, parts):
    wide = GROUP * HD
    slab = jax.ShapeDtypeStruct((wide + STAT, CHIP), BF16)
    return pl.pallas_call(
        functools.partial(memory_kernel, group),
        grid_spec=pltpu.PrefetchScalarGridSpec(
            num_scalar_prefetch=2,
            grid=(1,),
            in_specs=any_specs(8),
            out_specs=any_specs(4),
            scratch_shapes=[
                pltpu.VMEM((4, CHIP, wide), BF16),
                pltpu.VMEM((16, 2, 2, GROUP, BLK, HD), BF16),
                pltpu.VMEM((17, GROUP, HD, BLK), F32),
                pltpu.VMEM((17, GROUP, 1, BLK), F32),
                pltpu.VMEM((17, GROUP, 1, BLK), F32),
                pltpu.VMEM((4, wide + STAT, CHIP), BF16),
                pltpu.SemaphoreType.DMA((8,)),
                pltpu.SemaphoreType.DMA((4,)),
            ],
        ),
        out_shape=[slab] * 4,
        compiler_params=params(),
        cost_estimate=cost(32 * 4 * BLK * BLK * wide, 24 * 1024 * wide, 32 * 4 * BLK * BLK),
    )(*plan, *queries, *parts)


def merge_kernel(info, gate, *refs):
    y = info[1]
    groups = HEADS // GROUP
    own, oth = refs[-2:]
    local = refs[4 * groups : 4 * groups + 3]

    def merged(refs, shown, h, stats, share):
        logs = []
        for ref, show in zip(refs, shown):
            rows = ref[stats:, :].astype(F32)
            log = rows[3 * h : 3 * h + 1] + rows[3 * h + 1 : 3 * h + 2]
            log = log + rows[3 * h + 2 : 3 * h + 3]
            logs.append(log if show is None else jnp.where(show, log, NEG))
        top = functools.reduce(jnp.maximum, logs)
        weights = [jnp.exp2(log - top) for log in logs]
        scale = share / functools.reduce(jnp.add, weights)
        total = None
        for ref, weight in zip(refs, weights):
            term = ref[h * HD : (h + 1) * HD, :].astype(F32) * (weight * scale)
            total = term if total is None else total + term
        return total

    for h in range(HEADS):
        g = jax.nn.sigmoid(jnp.full((1, CHIP), gate[info[3] * HEADS + h], F32))
        first = h // GROUP * 4
        mix = merged(refs[first : first + 4], (None,) * 4, h % GROUP, GROUP * HD, g)
        mix = mix + merged(local, (None, y >= 1, y >= 2), h, FEAT, 1.0 - g)
        mix = mix.astype(BF16)
        own[:, h * HD : (h + 1) * HD] = mix[:, :TOK].T
        oth[:, h * HD : (h + 1) * HD] = mix[:, TOK:].T


def merge(info, gate, slabs):
    half = pl.BlockSpec((TOK, FEAT), lambda j, info, gate: (0, 0))
    return pl.pallas_call(
        merge_kernel,
        grid_spec=pltpu.PrefetchScalarGridSpec(
            num_scalar_prefetch=2,
            grid=(1,),
            in_specs=[pl.BlockSpec(s.shape, lambda j, info, gate: (0, 0)) for s in slabs],
            out_specs=[half] * 2,
        ),
        out_shape=[jax.ShapeDtypeStruct((TOK, FEAT), BF16)] * 2,
        compiler_params=params(),
        cost_estimate=cost(20 * SLAB * CHIP, 8 * 2 * SLAB * CHIP),
    )(info, gate, *slabs)


def output_kernel(info, own, oth, w_own, w_oth, out):
    total = dot(own[...], w_own[...], 1, 0) + dot(oth[...], w_oth[...], 1, 0)
    out[...] = total.astype(BF16)


def project_output(info, own, oth, w):
    width = w.shape[1]
    tile = 512
    half = pl.BlockSpec((TOK, FEAT), lambda j, info: (0, 0))
    return pl.pallas_call(
        output_kernel,
        grid_spec=pltpu.PrefetchScalarGridSpec(
            num_scalar_prefetch=1,
            grid=(width // tile,),
            in_specs=[
                half,
                half,
                pl.BlockSpec((FEAT, tile), lambda j, info: (info[3], j)),
                pl.BlockSpec((FEAT, tile), lambda j, info: (1 - info[3], j)),
            ],
            out_specs=pl.BlockSpec((TOK, tile), lambda j, info: (0, j)),
        ),
        out_shape=jax.ShapeDtypeStruct((TOK, width), BF16),
        compiler_params=params(),
        cost_estimate=cost(4 * TOK * FEAT * width, 4 * FEAT * width),
    )(info, own, oth, w, w)


def shards(tokens, block_ids, memory, w_query, w_key, w_value, w_out, gate_bias):
    mem = lax.axis_index("mem")
    seq = lax.axis_index("seq")
    y, c = seq // 2, seq % 2
    info = jnp.stack([mem // RING, y, mem % RING, c]).astype(jnp.int32)

    own = tokens[0]
    oth = send(own, core)
    ids_own = block_ids.reshape(1, 16)
    ids_chip = jnp.concatenate([ids_own, send(ids_own, core)], axis=1)
    ids_rows = jnp.zeros((STAT, FEAT), BF16).at[0:1, 0:32].set(ids_chip.astype(BF16))

    groups = HEADS // GROUP
    part = take_part(info, memory)
    near = [part] + [send(part, gather_move(0, d)) for d in (1, -1, 2)]

    query = project_query(info, own, oth, w_query, ids_rows)
    query1 = send(query, around(1))
    query2 = send(query, around(-1))
    k, v = project_keyvalue(info, own, oth, w_key, w_value)
    query3 = send(query1, around(1))
    queries = [query, query1, query2, query3]
    near = after(near, query, k)

    parts = []
    for g in range(groups):
        mine = jnp.concatenate([part[:, g] for part in near])
        below = send(mine, gather_move(1, 1))
        above = send(mine, gather_move(1, -1))
        far = send(below, gather_move(1, 1)) if g % 2 == 0 else send(above, gather_move(1, -1))
        parts.append((mine, below, above, far))

    (local0,) = local_attention(same_kernel, info, [query], k, v, 1)
    ids = jnp.concatenate([q[CHIP, 0:32] for q in queries]).astype(jnp.int32)
    plan = plan_units(info, ids)
    local1, local2 = local_attention(next_kernel, info, queries[1:], k, v, 2)
    local1 = send(local1, later1)
    local2 = send(local2, later2)

    slabs = []
    for g in range(groups):
        mine, one, two, far = memory_attention(g, plan, queries, parts[g])
        slabs += [mine, send(one, around(-1)), send(two, around(1)), send(far, around(2))]
    mix_own, mix_oth = merge(info, gate_bias, slabs + [local0, local1, local2])
    mix_oth = send(mix_oth, core)
    return project_output(info, mix_own, mix_oth, w_out)[None]


def solution(mesh):
    in_specs = (
        P("mem", "seq", None),
        P("mem", "seq", None),
        P("mem", None, None, None),
        P(),
        P(),
        P(),
        P(),
        P(),
    )
    out_specs = P("mem", "seq", None)
    return jax.shard_map(shards, mesh=mesh, in_specs=in_specs, out_specs=out_specs, check_vma=False)
```

```python
import functools

import jax
import jax.numpy as jnp
from jax import lax
from jax.experimental import pallas as pl
from jax.experimental.pallas import tpu as pltpu
from jax.sharding import PartitionSpec as P

RING = 4
HD = 128
FEAT = 512
HEADS = FEAT // HD
GROUP = 2
UNROLL = 4
TOK = 256
CHIP = 512
BLK = 128
STAT = 16
SLAB = FEAT + STAT
NEG = -1e30
F32 = jnp.float32
BF16 = jnp.bfloat16
LOG2E = 1.4426950408889634
VMEM = 24 * 1024 * 1024
WIDE_VMEM = 60 * 1024 * 1024


def index_of(x, y, z, c):
    return (y * 2 + c) * RING * RING + x * RING + z


def send(array, move):
    pairs = []
    for x in range(RING):
        for z in range(RING):
            for y in range(RING):
                for c in range(2):
                    to = move(x, y, z, c)
                    if to is not None:
                        pairs.append((index_of(x, y, z, c), index_of(*to)))
    return lax.ppermute(array, ("seq", "mem"), pairs)


def gather_move(phase, distance):
    def move(x, y, z, c):
        if (phase == 0) == (c == 0):
            return ((x + distance) % RING, y, z, c)
        return (x, y, (z + distance) % RING, c)

    return move


def around(distance):
    def move(x, y, z, c):
        return (x, (y + (distance if c == 0 else -distance)) % RING, z, c)

    return move


def later1(x, y, z, c):
    return (x, y + 1, z, c) if y + 1 < RING else None


def later2(x, y, z, c):
    return (x, y + 2, z, c) if y + 2 < RING else None


def core(x, y, z, c):
    return (x, y, z, 1 - c)


def params(limit=VMEM):
    return pltpu.CompilerParams(vmem_limit_bytes=limit)


def cost(flops, nbytes, trans=0):
    return pl.CostEstimate(flops=flops, bytes_accessed=nbytes, transcendentals=trans)


def any_specs(count):
    return [pl.BlockSpec(memory_space=pl.ANY)] * count


def dot(a, b, ca, cb):
    return lax.dot_general(a, b, (((ca,), (cb,)), ((), ())), preferred_element_type=F32)


def query_kernel(info, own, oth, w, ids, _, out):
    out[0:TOK, :] = dot(own[...], w[...], 1, 0).astype(BF16)
    out[TOK:CHIP, :] = dot(oth[...], w[...], 1, 0).astype(BF16)
    out[CHIP:, :] = ids[...]


def project_query(info, own, oth, w, ids, earlier):
    depth = own.shape[1]
    tile = 256
    steps = FEAT // tile
    whole = pl.BlockSpec((TOK, depth), lambda j, info: (0, 0))
    return pl.pallas_call(
        query_kernel,
        grid_spec=pltpu.PrefetchScalarGridSpec(
            num_scalar_prefetch=1,
            grid=(steps,),
            in_specs=[
                whole,
                whole,
                pl.BlockSpec((depth, tile), lambda j, info: (0, info[3] * steps + j)),
                pl.BlockSpec((STAT, tile), lambda j, info: (0, j)),
                pl.BlockSpec(memory_space=pl.ANY),
            ],
            out_specs=pl.BlockSpec((CHIP + STAT, tile), lambda j, info: (0, j)),
        ),
        out_shape=jax.ShapeDtypeStruct((CHIP + STAT, FEAT), BF16),
        compiler_params=params(WIDE_VMEM),
        cost_estimate=cost(2 * CHIP * depth * FEAT, 2 * depth * (FEAT + CHIP)),
    )(info, own, oth, w, ids, earlier)


def keyvalue_kernel(info, own, oth, wk, wv, _, k, v):
    for tok, place in ((own, slice(0, TOK)), (oth, slice(TOK, CHIP))):
        k[place, :] = dot(tok[...], wk[...], 1, 0).astype(BF16)
        v[:, place] = dot(tok[...], wv[...], 1, 0).astype(BF16).T


def project_keyvalue(info, own, oth, wk, wv, earlier):
    depth = own.shape[1]
    tile = 256
    steps = FEAT // tile
    whole = pl.BlockSpec((TOK, depth), lambda j, info: (0, 0))
    weight = pl.BlockSpec((depth, tile), lambda j, info: (0, info[3] * steps + j))
    result = pl.BlockSpec((CHIP, tile), lambda j, info: (0, j))
    return pl.pallas_call(
        keyvalue_kernel,
        grid_spec=pltpu.PrefetchScalarGridSpec(
            num_scalar_prefetch=1,
            grid=(steps,),
            in_specs=[whole, whole, weight, weight, pl.BlockSpec(memory_space=pl.ANY)],
            out_specs=[result, pl.BlockSpec((tile, CHIP), lambda j, info: (j, 0))],
        ),
        out_shape=[jax.ShapeDtypeStruct((CHIP, FEAT), BF16)] * 2,
        compiler_params=params(WIDE_VMEM),
        cost_estimate=cost(4 * CHIP * depth * FEAT, 2 * depth * (2 * FEAT + CHIP)),
    )(info, own, oth, wk, wv, earlier)


def split3(value):
    high = value.astype(BF16).astype(F32)
    rest = value - high
    mid = rest.astype(BF16).astype(F32)
    return high, mid, rest - mid


def pack_stats(values, width):
    row = lax.broadcasted_iota(jnp.int32, (STAT, width), 0)
    packed = jnp.zeros((STAT, width), F32)
    for h, value in enumerate(values):
        for i, part in enumerate(split3(value)):
            packed = jnp.where(row == 3 * h + i, part, packed)
    return packed.astype(BF16)


def local_block(distance, info, q, k, v, out):
    c = info[3]
    factor = HD ** -0.5 * LOG2E
    key = lax.broadcasted_iota(jnp.int32, (TOK, TOK), 0)
    ask = lax.broadcasted_iota(jnp.int32, (TOK, TOK), 1)
    valid = {0: ask >= key, 1: None, 2: ask < key}[distance]

    def half(place, halves):
        rows = slice(place * TOK, (place + 1) * TOK)
        stats = []
        for h in range(HEADS):
            cols = slice(h * HD, (h + 1) * HD)
            scores = []
            for i in halves:
                s = dot(k[i * TOK : (i + 1) * TOK, cols], q[rows, cols], 1, 1) * factor
                if i == place and valid is not None:
                    s = jnp.where(valid, s, NEG)
                scores.append(s)
            m = jnp.max(functools.reduce(jnp.maximum, scores), axis=0, keepdims=True)
            probs = [jnp.exp2(s - m) for s in scores]
            total = jnp.sum(functools.reduce(jnp.add, probs), axis=0, keepdims=True)
            parts = [
                dot(v[cols, i * TOK : (i + 1) * TOK], p.astype(BF16), 1, 0)
                for i, p in zip(halves, probs)
            ]
            mix = functools.reduce(jnp.add, parts)
            out[cols, rows] = (mix * (1.0 / total)).astype(BF16)
            stats.append(m + jnp.log2(total))
        out[FEAT:, rows] = pack_stats(stats, TOK)

    for place in range(2):
        if distance == 1:
            half(place, (0, 1))
            continue
        later = (place + c) == 1
        both = later if distance == 0 else jnp.logical_not(later)
        pl.when(both)(functools.partial(half, place, (0, 1)))
        pl.when(jnp.logical_not(both))(functools.partial(half, place, (place,)))


def same_kernel(info, q, k, v, out):
    local_block(0, info, q, k, v, out)


def next_kernel(info, q1, q2, q3, k, v, out1, out2):
    y, c = info[1], info[3]
    for near, here in ((q2, c == 0), (q1, c != 0)):

        @pl.when((y + 1 < RING) & here)
        def _():
            local_block(1, info, near, k, v, out1)

    @pl.when(y + 2 < RING)
    def _():
        local_block(2, info, q3, k, v, out2)


def held_specs(count):
    return [pl.BlockSpec(memory_space=pltpu.VMEM)] * count


def scalars(count):
    return [pl.BlockSpec(memory_space=pltpu.SMEM)] * count


def local_attention(kernel, info, queries, k, v, count):
    slab = jax.ShapeDtypeStruct((SLAB, CHIP), BF16)
    return pl.pallas_call(
        kernel,
        in_specs=scalars(1) + held_specs(len(queries) + 2),
        out_specs=held_specs(count),
        out_shape=[slab] * count,
        compiler_params=params(),
        cost_estimate=cost(4 * count * CHIP * CHIP * FEAT, 8 * CHIP * FEAT, 4 * CHIP * CHIP),
    )(info, *queries, k, v)


def part_kernel(info, mem, out, flag, held, sem):
    start = pl.multiple_of(info[3] * FEAT, FEAT)
    src = mem.at[pl.ds(2 * info[1], 2), :, :, pl.ds(start, FEAT)]
    copy = pltpu.make_async_copy(src, held, sem)
    copy.start()
    copy.wait()
    for block in range(2):
        for h in range(HEADS):
            cols = slice(h * HD, (h + 1) * HD)
            out[0, h // GROUP, block, 0, h % GROUP] = held[block, 0, :, cols]
            out[0, h // GROUP, block, 1, h % GROUP] = held[block, 1, :, cols].T
    flag[...] = jnp.zeros_like(flag)


def take_part(info, memory):
    shape = (1, HEADS // GROUP, 2, 2, GROUP, BLK, HD)
    return pl.pallas_call(
        part_kernel,
        grid_spec=pltpu.PrefetchScalarGridSpec(
            num_scalar_prefetch=1,
            grid=(1,),
            in_specs=[pl.BlockSpec(memory_space=pltpu.HBM)],
            out_specs=[
                pl.BlockSpec(shape, lambda j, info: (0,) * 7),
                pl.BlockSpec((8, HD), lambda j, info: (0, 0)),
            ],
            scratch_shapes=[
                pltpu.VMEM((2, 2, BLK, FEAT), BF16),
                pltpu.SemaphoreType.DMA,
            ],
        ),
        out_shape=[
            jax.ShapeDtypeStruct(shape, BF16),
            jax.ShapeDtypeStruct((8, HD), F32),
        ],
        compiler_params=params(WIDE_VMEM),
        cost_estimate=cost(0, 2**20),
    )(info, memory)


def join_kernel(group, *refs):
    near, out, sem = refs[:RING], refs[-2], refs[-1]
    copies = [
        pltpu.make_async_copy(ref.at[:, group], out.at[pl.ds(s, 1)], sem.at[s])
        for s, ref in enumerate(near)
    ]
    for copy in copies:
        copy.start()
    for copy in copies:
        copy.wait()


def join(group, near, *earlier):
    shape = (RING, *near[0].shape[2:])
    return pl.pallas_call(
        functools.partial(join_kernel, group),
        in_specs=any_specs(len(near) + len(earlier)),
        out_specs=pl.BlockSpec(memory_space=pl.ANY),
        out_shape=jax.ShapeDtypeStruct(shape, BF16),
        scratch_shapes=[pltpu.SemaphoreType.DMA((RING,))],
        compiler_params=params(),
        cost_estimate=cost(0, 2**20),
    )(*near, *earlier)


def plan_kernel(info, ids, slots, blocks):
    x, y, z, c = info[0], info[1], info[2], info[3]
    order = 120
    shift_x = jnp.where(c == 0, 0, 2)

    def look(n, used):
        count = used
        for t in range(8):
            ident = ids[n * 8 + t]
            ax = (order >> ((((ident >> 5) - x) & 3) * 2)) & 3
            az = (order >> (((((ident >> 3) & 3) - z) & 3) * 2)) & 3
            slot = (ax << shift_x) + (az << (2 - shift_x))
            slots[count] = slot * 2 + (ident & 1)
            blocks[count >> 1] = n
            count = count + (((ident >> 1) & 3) == y).astype(jnp.int32)
        slots[count] = 32
        return count + (count & 1)

    used = lax.fori_loop(0, 16, look, 0)
    units = used >> 1
    for u in range(UNROLL - 1):
        blocks[units + u] = 16
        slots[used + 2 * u] = 0
        slots[used + 2 * u + 1] = 32
    blocks[79] = (units + UNROLL - 1) // UNROLL


def plan_units(info, ids):
    smem = pl.BlockSpec(memory_space=pltpu.SMEM)
    return pl.pallas_call(
        plan_kernel,
        in_specs=[smem] * 2,
        out_specs=[smem] * 2,
        out_shape=[
            jax.ShapeDtypeStruct((144,), jnp.int32),
            jax.ShapeDtypeStruct((80,), jnp.int32),
        ],
        compiler_params=params(),
        cost_estimate=cost(1000, 1000),
    )(info, ids)


def memory_kernel(group, slots, blocks, *refs):
    queries, parts, outs = refs[:4], refs[4:8], refs[8:12]
    q, mem, acc, top, low, o, sem, osem = refs[12:]
    wide = GROUP * HD
    copies = [
        pltpu.make_async_copy(ref, mem.at[pl.ds(4 * s, 4)], sem.at[4 + s])
        for s, ref in enumerate(parts)
    ]
    for s, ref in enumerate(queries):
        src = ref.at[pl.ds(0, CHIP), pl.ds(group * wide, wide)]
        copies.append(pltpu.make_async_copy(src, q.at[s], sem.at[s]))
    for copy in copies:
        copy.start()

    acc[...] = jnp.zeros_like(acc)
    top[...] = jnp.full_like(top, NEG)
    low[...] = jnp.zeros_like(low)
    for copy in copies:
        copy.wait()

    factor = HD ** -0.5 * LOG2E

    def pair(i, carry):
        work = []
        for u in [UNROLL * i + k for k in range(UNROLL)]:
            n = blocks[u]
            from_q = jnp.minimum(n, 15)
            start = pl.multiple_of((from_q & 3) * BLK, BLK)
            second = slots[2 * u + 1]
            work.append((n, from_q >> 2, start, slots[2 * u], second & 31, second < 32))
        scores = {}
        for j, (n, s, start, one, two, full) in enumerate(work):
            for h in range(GROUP):
                keys = jnp.concatenate([mem[one >> 1, one & 1, 0, h], mem[two >> 1, two & 1, 0, h]], axis=0)
                qh = q[s, pl.ds(start, BLK), h * HD : (h + 1) * HD]
                scores[j, h] = dot(keys, qh, 1, 1) * factor
        for j, (n, s, start, one, two, full) in enumerate(work):
            for h in range(GROUP):
                first, last = scores[j, h][:BLK], scores[j, h][BLK:]
                last = jnp.where(full, last, NEG)
                m_old = top[n, h]
                m = jnp.max(jnp.maximum(first, last), axis=0, keepdims=True)
                m = jnp.maximum(m_old, m)
                p = jnp.concatenate([jnp.exp2(first - m), jnp.exp2(last - m)], axis=0)
                alpha = jnp.exp2(m_old - m)
                top[n, h] = m
                low[n, h] = low[n, h] * alpha + jnp.sum(p, axis=0, keepdims=True)
                values = jnp.concatenate([mem[one >> 1, one & 1, 1, h], mem[two >> 1, two & 1, 1, h]], axis=1)
                acc[n, h] = acc[n, h] * alpha + dot(values, p.astype(BF16), 1, 0)
        return carry

    lax.fori_loop(0, blocks[79], pair, 0)

    backs = [
        pltpu.make_async_copy(o.at[s], ref, osem.at[s]) for s, ref in enumerate(outs)
    ]
    for s in (3, 1, 2, 0):
        for b in range(4):
            n = s * 4 + b
            cols = slice(b * BLK, (b + 1) * BLK)
            stats = []
            for h in range(GROUP):
                total = low[n, h]
                some = total > 0.0
                total = jnp.where(some, total, 1.0)
                o[s, h * HD : (h + 1) * HD, cols] = (acc[n, h] * (1.0 / total)).astype(BF16)
                stats.append(jnp.where(some, top[n, h] + jnp.log2(total), NEG))
            o[s, wide:, cols] = pack_stats(stats, BLK)
        backs[s].start()
    for copy in backs:
        copy.wait()


def memory_attention(group, plan, queries, parts):
    wide = GROUP * HD
    slab = jax.ShapeDtypeStruct((wide + STAT, CHIP), BF16)
    return pl.pallas_call(
        functools.partial(memory_kernel, group),
        grid_spec=pltpu.PrefetchScalarGridSpec(
            num_scalar_prefetch=2,
            grid=(1,),
            in_specs=any_specs(8),
            out_specs=any_specs(4),
            scratch_shapes=[
                pltpu.VMEM((4, CHIP, wide), BF16),
                pltpu.VMEM((16, 2, 2, GROUP, BLK, HD), BF16),
                pltpu.VMEM((17, GROUP, HD, BLK), F32),
                pltpu.VMEM((17, GROUP, 1, BLK), F32),
                pltpu.VMEM((17, GROUP, 1, BLK), F32),
                pltpu.VMEM((4, wide + STAT, CHIP), BF16),
                pltpu.SemaphoreType.DMA((8,)),
                pltpu.SemaphoreType.DMA((4,)),
            ],
        ),
        out_shape=[slab] * 4,
        compiler_params=params(),
        cost_estimate=cost(32 * 4 * BLK * BLK * wide, 24 * 1024 * wide, 32 * 4 * BLK * BLK),
    )(*plan, *queries, *parts)


def merge_kernel(info, gate, *refs):
    y = info[1]
    groups = HEADS // GROUP
    own, oth = refs[-2:]
    local = refs[4 * groups : 4 * groups + 3]

    def merged(refs, shown, h, stats, share):
        logs = []
        for ref, show in zip(refs, shown):
            rows = ref[stats:, :].astype(F32)
            log = rows[3 * h : 3 * h + 1] + rows[3 * h + 1 : 3 * h + 2]
            log = log + rows[3 * h + 2 : 3 * h + 3]
            logs.append(log if show is None else jnp.where(show, log, NEG))
        top = functools.reduce(jnp.maximum, logs)
        weights = [jnp.exp2(log - top) for log in logs]
        scale = share / functools.reduce(jnp.add, weights)
        total = None
        for ref, weight in zip(refs, weights):
            term = ref[h * HD : (h + 1) * HD, :].astype(F32) * (weight * scale)
            total = term if total is None else total + term
        return total

    for h in range(HEADS):
        g = jax.nn.sigmoid(jnp.full((1, CHIP), gate[info[3] * HEADS + h], F32))
        first = h // GROUP * 4
        mix = merged(refs[first : first + 4], (None,) * 4, h % GROUP, GROUP * HD, g)
        mix = mix + merged(local, (None, y >= 1, y >= 2), h, FEAT, 1.0 - g)
        mix = mix.astype(BF16)
        own[:, h * HD : (h + 1) * HD] = mix[:, :TOK].T
        oth[:, h * HD : (h + 1) * HD] = mix[:, TOK:].T


def merge(info, gate, slabs):
    return pl.pallas_call(
        merge_kernel,
        in_specs=scalars(2) + held_specs(len(slabs)),
        out_specs=held_specs(2),
        out_shape=[jax.ShapeDtypeStruct((TOK, FEAT), BF16)] * 2,
        compiler_params=params(),
        cost_estimate=cost(20 * SLAB * CHIP, 8 * 2 * SLAB * CHIP),
    )(info, gate, *slabs)


def output_kernel(info, own, oth, w, out):
    c = info[3]
    mine = pl.ds(pl.multiple_of(c * FEAT, FEAT), FEAT)
    other = pl.ds(pl.multiple_of((1 - c) * FEAT, FEAT), FEAT)
    tile = 512
    for j in range(out.shape[1] // tile):
        cols = slice(j * tile, (j + 1) * tile)
        total = dot(own[...], w[mine, cols], 1, 0) + dot(oth[...], w[other, cols], 1, 0)
        out[:, cols] = total.astype(BF16)


def project_output(info, own, oth, w):
    def whole(array):
        return pl.BlockSpec(array.shape, lambda j, info: (0, 0))

    result = jax.ShapeDtypeStruct((TOK, w.shape[1]), BF16)
    return pl.pallas_call(
        output_kernel,
        grid_spec=pltpu.PrefetchScalarGridSpec(
            num_scalar_prefetch=1,
            grid=(1,),
            in_specs=[whole(own), whole(oth), whole(w)],
            out_specs=whole(result),
        ),
        out_shape=result,
        compiler_params=params(),
        cost_estimate=cost(4 * TOK * FEAT * w.shape[1], 4 * FEAT * w.shape[1]),
    )(info, own, oth, w)


def shards(tokens, block_ids, memory, w_query, w_key, w_value, w_out, gate_bias):
    mem = lax.axis_index("mem")
    seq = lax.axis_index("seq")
    y, c = seq // 2, seq % 2
    info = jnp.stack([mem // RING, y, mem % RING, c]).astype(jnp.int32)

    own = tokens[0]
    oth = send(own, core)
    ids_own = block_ids.reshape(1, 16)
    ids_chip = jnp.concatenate([ids_own, send(ids_own, core)], axis=1)
    ids_rows = jnp.zeros((STAT, FEAT), BF16).at[0:1, 0:32].set(ids_chip.astype(BF16))

    groups = HEADS // GROUP
    part, taken = take_part(info, memory)
    near = [part] + [send(part, gather_move(0, d)) for d in (1, -1, 2)]

    query = project_query(info, own, oth, w_query, ids_rows, taken)
    query1 = send(query, around(1))
    query2 = send(query, around(-1))
    k, v = project_keyvalue(info, own, oth, w_key, w_value, query)
    query3 = send(query1, around(1))
    queries = [query, query1, query2, query3]

    parts = []
    for g in range(groups):
        mine = join(g, near, *((query1, k) if g == 1 else ()))
        below = send(mine, gather_move(1, 1))
        above = send(mine, gather_move(1, -1))
        far = send(below, gather_move(1, 1)) if g % 2 == 0 else send(above, gather_move(1, -1))
        parts.append((mine, below, above, far))

    (local0,) = local_attention(same_kernel, info, [query], k, v, 1)
    ids = jnp.concatenate([q[CHIP, 0:32] for q in queries]).astype(jnp.int32)
    plan = plan_units(info, ids)
    local1, local2 = local_attention(next_kernel, info, queries[1:], k, v, 2)
    local1 = send(local1, later1)
    local2 = send(local2, later2)

    slabs = []
    for g in range(groups):
        mine, one, two, far = memory_attention(g, plan, queries, parts[g])
        slabs += [mine, send(one, around(-1)), send(two, around(1)), send(far, around(2))]
    mix_own, mix_oth = merge(info, gate_bias, slabs + [local0, local1, local2])
    mix_oth = send(mix_oth, core)
    return project_output(info, mix_own, mix_oth, w_out)[None]


def solution(mesh):
    in_specs = (
        P("mem", "seq", None),
        P("mem", "seq", None),
        P("mem", None, None, None),
        P(),
        P(),
        P(),
        P(),
        P(),
    )
    out_specs = P("mem", "seq", None)
    return jax.shard_map(shards, mesh=mesh, in_specs=in_specs, out_specs=out_specs, check_vma=False)
```

```python
import functools

import jax
import jax.numpy as jnp
from jax import lax
from jax.experimental import pallas as pl
from jax.experimental.pallas import tpu as pltpu
from jax.sharding import PartitionSpec as P

RING = 4
HD = 128
FEAT = 512
HEADS = FEAT // HD
GROUP = 2
UNROLL = 4
TOK = 256
CHIP = 512
BLK = 128
STAT = 16
SLAB = FEAT + STAT
NEG = -1e30
F32 = jnp.float32
BF16 = jnp.bfloat16
LOG2E = 1.4426950408889634
VMEM = 24 * 1024 * 1024
WIDE_VMEM = 60 * 1024 * 1024


def index_of(x, y, z, c):
    return (y * 2 + c) * RING * RING + x * RING + z


def send(array, move):
    pairs = []
    for x in range(RING):
        for z in range(RING):
            for y in range(RING):
                for c in range(2):
                    to = move(x, y, z, c)
                    if to is not None:
                        pairs.append((index_of(x, y, z, c), index_of(*to)))
    return lax.ppermute(array, ("seq", "mem"), pairs)


def gather_move(phase, distance):
    def move(x, y, z, c):
        if (phase == 0) == (c == 0):
            return ((x + distance) % RING, y, z, c)
        return (x, y, (z + distance) % RING, c)

    return move


def around(distance):
    def move(x, y, z, c):
        return (x, (y + (distance if c == 0 else -distance)) % RING, z, c)

    return move


def later1(x, y, z, c):
    return (x, y + 1, z, c) if y + 1 < RING else None


def later2(x, y, z, c):
    return (x, y + 2, z, c) if y + 2 < RING else None


def core(x, y, z, c):
    return (x, y, z, 1 - c)


def params(limit=VMEM):
    return pltpu.CompilerParams(vmem_limit_bytes=limit)


def cost(flops, nbytes, trans=0):
    return pl.CostEstimate(flops=flops, bytes_accessed=nbytes, transcendentals=trans)


def any_specs(count):
    return [pl.BlockSpec(memory_space=pl.ANY)] * count


def dot(a, b, ca, cb):
    return lax.dot_general(a, b, (((ca,), (cb,)), ((), ())), preferred_element_type=F32)


def query_kernel(info, own, oth, w, ids, _, out):
    out[0:TOK, :] = dot(own[...], w[...], 1, 0).astype(BF16)
    out[TOK:CHIP, :] = dot(oth[...], w[...], 1, 0).astype(BF16)
    out[CHIP:, :] = ids[...]


def project_query(info, own, oth, w, ids, earlier):
    depth = own.shape[1]
    tile = 256
    steps = FEAT // tile
    whole = pl.BlockSpec((TOK, depth), lambda j, info: (0, 0))
    return pl.pallas_call(
        query_kernel,
        grid_spec=pltpu.PrefetchScalarGridSpec(
            num_scalar_prefetch=1,
            grid=(steps,),
            in_specs=[
                whole,
                whole,
                pl.BlockSpec((depth, tile), lambda j, info: (0, info[3] * steps + j)),
                pl.BlockSpec((STAT, tile), lambda j, info: (0, j)),
                pl.BlockSpec(memory_space=pl.ANY),
            ],
            out_specs=pl.BlockSpec((CHIP + STAT, tile), lambda j, info: (0, j)),
        ),
        out_shape=jax.ShapeDtypeStruct((CHIP + STAT, FEAT), BF16),
        compiler_params=params(WIDE_VMEM),
        cost_estimate=cost(2 * CHIP * depth * FEAT, 2 * depth * (FEAT + CHIP)),
    )(info, own, oth, w, ids, earlier)


def keyvalue_kernel(info, own, oth, wk, wv, _, k, v):
    for tok, place in ((own, slice(0, TOK)), (oth, slice(TOK, CHIP))):
        k[place, :] = dot(tok[...], wk[...], 1, 0).astype(BF16)
        v[:, place] = dot(tok[...], wv[...], 1, 0).astype(BF16).T


def project_keyvalue(info, own, oth, wk, wv, earlier):
    depth = own.shape[1]
    tile = 256
    steps = FEAT // tile
    whole = pl.BlockSpec((TOK, depth), lambda j, info: (0, 0))
    weight = pl.BlockSpec((depth, tile), lambda j, info: (0, info[3] * steps + j))
    result = pl.BlockSpec((CHIP, tile), lambda j, info: (0, j))
    return pl.pallas_call(
        keyvalue_kernel,
        grid_spec=pltpu.PrefetchScalarGridSpec(
            num_scalar_prefetch=1,
            grid=(steps,),
            in_specs=[whole, whole, weight, weight, pl.BlockSpec(memory_space=pl.ANY)],
            out_specs=[result, pl.BlockSpec((tile, CHIP), lambda j, info: (j, 0))],
        ),
        out_shape=[jax.ShapeDtypeStruct((CHIP, FEAT), BF16)] * 2,
        compiler_params=params(WIDE_VMEM),
        cost_estimate=cost(4 * CHIP * depth * FEAT, 2 * depth * (2 * FEAT + CHIP)),
    )(info, own, oth, wk, wv, earlier)


def split3(value):
    high = value.astype(BF16).astype(F32)
    rest = value - high
    mid = rest.astype(BF16).astype(F32)
    return high, mid, rest - mid


def pack_stats(values, width):
    row = lax.broadcasted_iota(jnp.int32, (STAT, width), 0)
    packed = jnp.zeros((STAT, width), F32)
    for h, value in enumerate(values):
        for i, part in enumerate(split3(value)):
            packed = jnp.where(row == 3 * h + i, part, packed)
    return packed.astype(BF16)


def local_block(distance, info, q, k, v, out):
    c = info[3]
    factor = HD ** -0.5 * LOG2E
    key = lax.broadcasted_iota(jnp.int32, (TOK, TOK), 0)
    ask = lax.broadcasted_iota(jnp.int32, (TOK, TOK), 1)
    valid = {0: ask >= key, 1: None, 2: ask < key}[distance]

    def half(place, halves):
        rows = slice(place * TOK, (place + 1) * TOK)
        stats = []
        for h in range(HEADS):
            cols = slice(h * HD, (h + 1) * HD)
            scores = []
            for i in halves:
                s = dot(k[i * TOK : (i + 1) * TOK, cols], q[rows, cols], 1, 1) * factor
                if i == place and valid is not None:
                    s = jnp.where(valid, s, NEG)
                scores.append(s)
            m = jnp.max(functools.reduce(jnp.maximum, scores), axis=0, keepdims=True)
            probs = [jnp.exp2(s - m) for s in scores]
            total = jnp.sum(functools.reduce(jnp.add, probs), axis=0, keepdims=True)
            parts = [
                dot(v[cols, i * TOK : (i + 1) * TOK], p.astype(BF16), 1, 0)
                for i, p in zip(halves, probs)
            ]
            mix = functools.reduce(jnp.add, parts)
            out[cols, rows] = (mix * (1.0 / total)).astype(BF16)
            stats.append(m + jnp.log2(total))
        out[FEAT:, rows] = pack_stats(stats, TOK)

    for place in range(2):
        if distance == 1:
            half(place, (0, 1))
            continue
        later = (place + c) == 1
        both = later if distance == 0 else jnp.logical_not(later)
        pl.when(both)(functools.partial(half, place, (0, 1)))
        pl.when(jnp.logical_not(both))(functools.partial(half, place, (place,)))


def same_kernel(info, q, k, v, out):
    local_block(0, info, q, k, v, out)


def next_kernel(info, q1, q2, k, v, out):
    y, c = info[1], info[3]
    for near, here in ((q2, c == 0), (q1, c != 0)):

        @pl.when((y + 1 < RING) & here)
        def _():
            local_block(1, info, near, k, v, out)


def second_kernel(info, q3, k, v, _, out):
    @pl.when(info[1] + 2 < RING)
    def _():
        local_block(2, info, q3, k, v, out)


def held_specs(count):
    return [pl.BlockSpec(memory_space=pltpu.VMEM)] * count


def scalars(count):
    return [pl.BlockSpec(memory_space=pltpu.SMEM)] * count


def local_attention(kernel, info, queries, k, v, *earlier):
    count = 1
    slab = jax.ShapeDtypeStruct((SLAB, CHIP), BF16)
    return pl.pallas_call(
        kernel,
        in_specs=scalars(1) + held_specs(len(queries) + 2) + any_specs(len(earlier)),
        out_specs=held_specs(count),
        out_shape=[slab] * count,
        compiler_params=params(),
        cost_estimate=cost(4 * count * CHIP * CHIP * FEAT, 8 * CHIP * FEAT, 4 * CHIP * CHIP),
    )(info, *queries, k, v, *earlier)


def part_kernel(info, mem, out, flag, held, sem):
    start = pl.multiple_of(info[3] * FEAT, FEAT)
    src = mem.at[pl.ds(2 * info[1], 2), :, :, pl.ds(start, FEAT)]
    copy = pltpu.make_async_copy(src, held, sem)
    copy.start()
    copy.wait()
    for block in range(2):
        for h in range(HEADS):
            cols = slice(h * HD, (h + 1) * HD)
            out[0, h // GROUP, block, 0, h % GROUP] = held[block, 0, :, cols]
            out[0, h // GROUP, block, 1, h % GROUP] = held[block, 1, :, cols].T
    flag[...] = jnp.zeros_like(flag)


def take_part(info, memory):
    shape = (1, HEADS // GROUP, 2, 2, GROUP, BLK, HD)
    return pl.pallas_call(
        part_kernel,
        grid_spec=pltpu.PrefetchScalarGridSpec(
            num_scalar_prefetch=1,
            grid=(1,),
            in_specs=[pl.BlockSpec(memory_space=pltpu.HBM)],
            out_specs=[
                pl.BlockSpec(shape, lambda j, info: (0,) * 7),
                pl.BlockSpec((8, HD), lambda j, info: (0, 0)),
            ],
            scratch_shapes=[
                pltpu.VMEM((2, 2, BLK, FEAT), BF16),
                pltpu.SemaphoreType.DMA,
            ],
        ),
        out_shape=[
            jax.ShapeDtypeStruct(shape, BF16),
            jax.ShapeDtypeStruct((8, HD), F32),
        ],
        compiler_params=params(WIDE_VMEM),
        cost_estimate=cost(0, 2**20),
    )(info, memory)


def join_kernel(group, *refs):
    near, out, sem = refs[:RING], refs[-2], refs[-1]
    copies = [
        pltpu.make_async_copy(ref.at[:, group], out.at[pl.ds(s, 1)], sem.at[s])
        for s, ref in enumerate(near)
    ]
    for copy in copies:
        copy.start()
    for copy in copies:
        copy.wait()


def join(group, near, *earlier):
    shape = (RING, *near[0].shape[2:])
    return pl.pallas_call(
        functools.partial(join_kernel, group),
        in_specs=any_specs(len(near) + len(earlier)),
        out_specs=pl.BlockSpec(memory_space=pl.ANY),
        out_shape=jax.ShapeDtypeStruct(shape, BF16),
        scratch_shapes=[pltpu.SemaphoreType.DMA((RING,))],
        compiler_params=params(),
        cost_estimate=cost(0, 2**20),
    )(*near, *earlier)


def plan_kernel(info, ids, slots, blocks):
    x, y, z, c = info[0], info[1], info[2], info[3]
    order = 120
    shift_x = jnp.where(c == 0, 0, 2)

    def look(n, used):
        count = used
        for t in range(8):
            ident = ids[n * 8 + t]
            ax = (order >> ((((ident >> 5) - x) & 3) * 2)) & 3
            az = (order >> (((((ident >> 3) & 3) - z) & 3) * 2)) & 3
            slot = (ax << shift_x) + (az << (2 - shift_x))
            slots[count] = slot * 2 + (ident & 1)
            blocks[count >> 1] = n
            count = count + (((ident >> 1) & 3) == y).astype(jnp.int32)
        slots[count] = 32
        return count + (count & 1)

    used = lax.fori_loop(0, 16, look, 0)
    units = used >> 1
    for u in range(UNROLL - 1):
        blocks[units + u] = 16
        slots[used + 2 * u] = 0
        slots[used + 2 * u + 1] = 32
    blocks[79] = (units + UNROLL - 1) // UNROLL


def plan_units(info, ids):
    smem = pl.BlockSpec(memory_space=pltpu.SMEM)
    return pl.pallas_call(
        plan_kernel,
        in_specs=[smem] * 2,
        out_specs=[smem] * 2,
        out_shape=[
            jax.ShapeDtypeStruct((144,), jnp.int32),
            jax.ShapeDtypeStruct((80,), jnp.int32),
        ],
        compiler_params=params(),
        cost_estimate=cost(1000, 1000),
    )(info, ids)


def memory_kernel(group, slots, blocks, *refs):
    queries, parts, outs = refs[:4], refs[4:8], refs[8:12]
    q, mem, acc, top, low, o, sem, osem = refs[12:]
    wide = GROUP * HD
    copies = [
        pltpu.make_async_copy(ref, mem.at[pl.ds(4 * s, 4)], sem.at[4 + s])
        for s, ref in enumerate(parts)
    ]
    for s, ref in enumerate(queries):
        src = ref.at[pl.ds(0, CHIP), pl.ds(group * wide, wide)]
        copies.append(pltpu.make_async_copy(src, q.at[s], sem.at[s]))
    for copy in copies:
        copy.start()

    acc[...] = jnp.zeros_like(acc)
    top[...] = jnp.full_like(top, NEG)
    low[...] = jnp.zeros_like(low)
    for copy in copies:
        copy.wait()

    factor = HD ** -0.5 * LOG2E

    def pair(i, carry):
        work = []
        for u in [UNROLL * i + k for k in range(UNROLL)]:
            n = blocks[u]
            from_q = jnp.minimum(n, 15)
            start = pl.multiple_of((from_q & 3) * BLK, BLK)
            second = slots[2 * u + 1]
            work.append((n, from_q >> 2, start, slots[2 * u], second & 31, second < 32))
        scores = {}
        for j, (n, s, start, one, two, full) in enumerate(work):
            for h in range(GROUP):
                keys = jnp.concatenate([mem[one >> 1, one & 1, 0, h], mem[two >> 1, two & 1, 0, h]], axis=0)
                qh = q[s, pl.ds(start, BLK), h * HD : (h + 1) * HD]
                scores[j, h] = dot(keys, qh, 1, 1) * factor
        for j, (n, s, start, one, two, full) in enumerate(work):
            for h in range(GROUP):
                first, last = scores[j, h][:BLK], scores[j, h][BLK:]
                last = jnp.where(full, last, NEG)
                m_old = top[n, h]
                m = jnp.max(jnp.maximum(first, last), axis=0, keepdims=True)
                m = jnp.maximum(m_old, m)
                p = jnp.concatenate([jnp.exp2(first - m), jnp.exp2(last - m)], axis=0)
                alpha = jnp.exp2(m_old - m)
                top[n, h] = m
                low[n, h] = low[n, h] * alpha + jnp.sum(p, axis=0, keepdims=True)
                values = jnp.concatenate([mem[one >> 1, one & 1, 1, h], mem[two >> 1, two & 1, 1, h]], axis=1)
                acc[n, h] = acc[n, h] * alpha + dot(values, p.astype(BF16), 1, 0)
        return carry

    lax.fori_loop(0, blocks[79], pair, 0)

    backs = [
        pltpu.make_async_copy(o.at[s], ref, osem.at[s]) for s, ref in enumerate(outs)
    ]
    for s in (3, 1, 2, 0):
        for b in range(4):
            n = s * 4 + b
            cols = slice(b * BLK, (b + 1) * BLK)
            stats = []
            for h in range(GROUP):
                total = low[n, h]
                some = total > 0.0
                total = jnp.where(some, total, 1.0)
                o[s, h * HD : (h + 1) * HD, cols] = (acc[n, h] * (1.0 / total)).astype(BF16)
                stats.append(jnp.where(some, top[n, h] + jnp.log2(total), NEG))
            o[s, wide:, cols] = pack_stats(stats, BLK)
        backs[s].start()
    for copy in backs:
        copy.wait()


def memory_attention(group, plan, queries, parts):
    wide = GROUP * HD
    slab = jax.ShapeDtypeStruct((wide + STAT, CHIP), BF16)
    return pl.pallas_call(
        functools.partial(memory_kernel, group),
        grid_spec=pltpu.PrefetchScalarGridSpec(
            num_scalar_prefetch=2,
            grid=(1,),
            in_specs=any_specs(8),
            out_specs=any_specs(4),
            scratch_shapes=[
                pltpu.VMEM((4, CHIP, wide), BF16),
                pltpu.VMEM((16, 2, 2, GROUP, BLK, HD), BF16),
                pltpu.VMEM((17, GROUP, HD, BLK), F32),
                pltpu.VMEM((17, GROUP, 1, BLK), F32),
                pltpu.VMEM((17, GROUP, 1, BLK), F32),
                pltpu.VMEM((4, wide + STAT, CHIP), BF16),
                pltpu.SemaphoreType.DMA((8,)),
                pltpu.SemaphoreType.DMA((4,)),
            ],
        ),
        out_shape=[slab] * 4,
        compiler_params=params(),
        cost_estimate=cost(32 * 4 * BLK * BLK * wide, 24 * 1024 * wide, 32 * 4 * BLK * BLK),
    )(*plan, *queries, *parts)


def merge_kernel(info, gate, *refs):
    y = info[1]
    groups = HEADS // GROUP
    own, oth = refs[-2:]
    local = refs[4 * groups : 4 * groups + 3]

    def merged(refs, shown, h, stats, share):
        logs = []
        for ref, show in zip(refs, shown):
            rows = ref[stats:, :].astype(F32)
            log = rows[3 * h : 3 * h + 1] + rows[3 * h + 1 : 3 * h + 2]
            log = log + rows[3 * h + 2 : 3 * h + 3]
            logs.append(log if show is None else jnp.where(show, log, NEG))
        top = functools.reduce(jnp.maximum, logs)
        weights = [jnp.exp2(log - top) for log in logs]
        scale = share / functools.reduce(jnp.add, weights)
        total = None
        for ref, weight in zip(refs, weights):
            term = ref[h * HD : (h + 1) * HD, :].astype(F32) * (weight * scale)
            total = term if total is None else total + term
        return total

    for h in range(HEADS):
        g = jax.nn.sigmoid(jnp.full((1, CHIP), gate[info[3] * HEADS + h], F32))
        first = h // GROUP * 4
        mix = merged(refs[first : first + 4], (None,) * 4, h % GROUP, GROUP * HD, g)
        mix = mix + merged(local, (None, y >= 1, y >= 2), h, FEAT, 1.0 - g)
        mix = mix.astype(BF16)
        own[:, h * HD : (h + 1) * HD] = mix[:, :TOK].T
        oth[:, h * HD : (h + 1) * HD] = mix[:, TOK:].T


def merge(info, gate, slabs):
    return pl.pallas_call(
        merge_kernel,
        in_specs=scalars(2) + held_specs(len(slabs)),
        out_specs=held_specs(2),
        out_shape=[jax.ShapeDtypeStruct((TOK, FEAT), BF16)] * 2,
        compiler_params=params(),
        cost_estimate=cost(20 * SLAB * CHIP, 8 * 2 * SLAB * CHIP),
    )(info, gate, *slabs)


def output_kernel(info, own, oth, w, out):
    c = info[3]
    mine = pl.ds(pl.multiple_of(c * FEAT, FEAT), FEAT)
    other = pl.ds(pl.multiple_of((1 - c) * FEAT, FEAT), FEAT)
    tile = 512
    for j in range(out.shape[1] // tile):
        cols = slice(j * tile, (j + 1) * tile)
        total = dot(own[...], w[mine, cols], 1, 0) + dot(oth[...], w[other, cols], 1, 0)
        out[:, cols] = total.astype(BF16)


def project_output(info, own, oth, w):
    def whole(array):
        return pl.BlockSpec(array.shape, lambda j, info: (0, 0))

    result = jax.ShapeDtypeStruct((TOK, w.shape[1]), BF16)
    return pl.pallas_call(
        output_kernel,
        grid_spec=pltpu.PrefetchScalarGridSpec(
            num_scalar_prefetch=1,
            grid=(1,),
            in_specs=[whole(own), whole(oth), whole(w)],
            out_specs=whole(result),
        ),
        out_shape=result,
        compiler_params=params(),
        cost_estimate=cost(4 * TOK * FEAT * w.shape[1], 4 * FEAT * w.shape[1]),
    )(info, own, oth, w)


def shards(tokens, block_ids, memory, w_query, w_key, w_value, w_out, gate_bias):
    mem = lax.axis_index("mem")
    seq = lax.axis_index("seq")
    y, c = seq // 2, seq % 2
    info = jnp.stack([mem // RING, y, mem % RING, c]).astype(jnp.int32)

    own = tokens[0]
    oth = send(own, core)
    ids_own = block_ids.reshape(1, 16)
    ids_chip = jnp.concatenate([ids_own, send(ids_own, core)], axis=1)
    ids_rows = jnp.zeros((STAT, FEAT), BF16).at[0:1, 0:32].set(ids_chip.astype(BF16))

    groups = HEADS // GROUP
    part, taken = take_part(info, memory)
    near = [part] + [send(part, gather_move(0, d)) for d in (1, -1, 2)]

    query = project_query(info, own, oth, w_query, ids_rows, taken)
    query1 = send(query, around(1))
    query2 = send(query, around(-1))
    k, v = project_keyvalue(info, own, oth, w_key, w_value, query)
    query3 = send(query1, around(1))
    queries = [query, query1, query2, query3]

    parts = []
    for g in range(groups):
        mine = join(g, near, *((query1, k) if g == 1 else ()))
        below = send(mine, gather_move(1, 1))
        above = send(mine, gather_move(1, -1))
        far = send(below, gather_move(1, 1)) if g % 2 == 0 else send(above, gather_move(1, -1))
        parts.append((mine, below, above, far))

    (local0,) = local_attention(same_kernel, info, [query], k, v)
    ids = jnp.concatenate([q[CHIP, 0:32] for q in queries]).astype(jnp.int32)
    plan = plan_units(info, ids)
    (local1,) = local_attention(next_kernel, info, queries[1:3], k, v)
    (local2,) = local_attention(second_kernel, info, queries[3:], k, v, local1)
    local1 = send(local1, later1)
    local2 = send(local2, later2)

    slabs = []
    for g in range(groups):
        mine, one, two, far = memory_attention(g, plan, queries, parts[g])
        slabs += [mine, send(one, around(-1)), send(two, around(1)), send(far, around(2))]
    mix_own, mix_oth = merge(info, gate_bias, slabs + [local0, local1, local2])
    mix_oth = send(mix_oth, core)
    return project_output(info, mix_own, mix_oth, w_out)[None]


def solution(mesh):
    in_specs = (
        P("mem", "seq", None),
        P("mem", "seq", None),
        P("mem", None, None, None),
        P(),
        P(),
        P(),
        P(),
        P(),
    )
    out_specs = P("mem", "seq", None)
    return jax.shard_map(shards, mesh=mesh, in_specs=in_specs, out_specs=out_specs, check_vma=False)
```

```python
import functools

import jax
import jax.numpy as jnp
from jax import lax
from jax.experimental import pallas as pl
from jax.experimental.pallas import tpu as pltpu
from jax.sharding import PartitionSpec as P

RING = 4
HD = 128
FEAT = 512
HEADS = FEAT // HD
GROUP = 2
UNROLL = 4
TOK = 256
CHIP = 512
BLK = 128
STAT = 16
SLAB = FEAT + STAT
NEG = -1e30
F32 = jnp.float32
BF16 = jnp.bfloat16
LOG2E = 1.4426950408889634
VMEM = 24 * 1024 * 1024
WIDE_VMEM = 60 * 1024 * 1024


def index_of(x, y, z, c):
    return (y * 2 + c) * RING * RING + x * RING + z


def send(array, move):
    pairs = []
    for x in range(RING):
        for z in range(RING):
            for y in range(RING):
                for c in range(2):
                    to = move(x, y, z, c)
                    if to is not None:
                        pairs.append((index_of(x, y, z, c), index_of(*to)))
    return lax.ppermute(array, ("seq", "mem"), pairs)


def gather_move(phase, distance):
    def move(x, y, z, c):
        if (phase == 0) == (c == 0):
            return ((x + distance) % RING, y, z, c)
        return (x, y, (z + distance) % RING, c)

    return move


def around(distance):
    def move(x, y, z, c):
        return (x, (y + (distance if c == 0 else -distance)) % RING, z, c)

    return move


def later1(x, y, z, c):
    return (x, y + 1, z, c) if y + 1 < RING else None


def later2(x, y, z, c):
    return (x, y + 2, z, c) if y + 2 < RING else None


def core(x, y, z, c):
    return (x, y, z, 1 - c)


def params(limit=VMEM):
    return pltpu.CompilerParams(vmem_limit_bytes=limit)


def cost(flops, nbytes, trans=0):
    return pl.CostEstimate(flops=flops, bytes_accessed=nbytes, transcendentals=trans)


def any_specs(count):
    return [pl.BlockSpec(memory_space=pl.ANY)] * count


def dot(a, b, ca, cb):
    return lax.dot_general(a, b, (((ca,), (cb,)), ((), ())), preferred_element_type=F32)


def query_kernel(info, own, oth, w, ids, _, out):
    out[0:TOK, :] = dot(own[...], w[...], 1, 0).astype(BF16)
    out[TOK:CHIP, :] = dot(oth[...], w[...], 1, 0).astype(BF16)
    out[CHIP:, :] = ids[...]


def project_query(info, own, oth, w, ids, earlier):
    depth = own.shape[1]
    tile = 256
    steps = FEAT // tile
    whole = pl.BlockSpec((TOK, depth), lambda j, info: (0, 0))
    return pl.pallas_call(
        query_kernel,
        grid_spec=pltpu.PrefetchScalarGridSpec(
            num_scalar_prefetch=1,
            grid=(steps,),
            in_specs=[
                whole,
                whole,
                pl.BlockSpec((depth, tile), lambda j, info: (0, info[3] * steps + j)),
                pl.BlockSpec((STAT, tile), lambda j, info: (0, j)),
                pl.BlockSpec(memory_space=pl.ANY),
            ],
            out_specs=pl.BlockSpec((CHIP + STAT, tile), lambda j, info: (0, j)),
        ),
        out_shape=jax.ShapeDtypeStruct((CHIP + STAT, FEAT), BF16),
        compiler_params=params(WIDE_VMEM),
        cost_estimate=cost(2 * CHIP * depth * FEAT, 2 * depth * (FEAT + CHIP)),
    )(info, own, oth, w, ids, earlier)


def keyvalue_kernel(info, own, oth, wk, wv, _, k, v):
    for tok, place in ((own, slice(0, TOK)), (oth, slice(TOK, CHIP))):
        k[place, :] = dot(tok[...], wk[...], 1, 0).astype(BF16)
        v[:, place] = dot(tok[...], wv[...], 1, 0).astype(BF16).T


def project_keyvalue(info, own, oth, wk, wv, earlier):
    depth = own.shape[1]
    tile = 256
    steps = FEAT // tile
    whole = pl.BlockSpec((TOK, depth), lambda j, info: (0, 0))
    weight = pl.BlockSpec((depth, tile), lambda j, info: (0, info[3] * steps + j))
    result = pl.BlockSpec((CHIP, tile), lambda j, info: (0, j))
    return pl.pallas_call(
        keyvalue_kernel,
        grid_spec=pltpu.PrefetchScalarGridSpec(
            num_scalar_prefetch=1,
            grid=(steps,),
            in_specs=[whole, whole, weight, weight, pl.BlockSpec(memory_space=pl.ANY)],
            out_specs=[result, pl.BlockSpec((tile, CHIP), lambda j, info: (j, 0))],
        ),
        out_shape=[jax.ShapeDtypeStruct((CHIP, FEAT), BF16)] * 2,
        compiler_params=params(WIDE_VMEM),
        cost_estimate=cost(4 * CHIP * depth * FEAT, 2 * depth * (2 * FEAT + CHIP)),
    )(info, own, oth, wk, wv, earlier)


def split3(value):
    high = value.astype(BF16).astype(F32)
    rest = value - high
    mid = rest.astype(BF16).astype(F32)
    return high, mid, rest - mid


def pack_stats(values, width):
    row = lax.broadcasted_iota(jnp.int32, (STAT, width), 0)
    packed = jnp.zeros((STAT, width), F32)
    for h, value in enumerate(values):
        for i, part in enumerate(split3(value)):
            packed = jnp.where(row == 3 * h + i, part, packed)
    return packed.astype(BF16)


def local_block(distance, info, q, k, v, out):
    c = info[3]
    factor = HD ** -0.5 * LOG2E
    key = lax.broadcasted_iota(jnp.int32, (TOK, TOK), 0)
    ask = lax.broadcasted_iota(jnp.int32, (TOK, TOK), 1)
    valid = {0: ask >= key, 1: None, 2: ask < key}[distance]

    def half(place, halves):
        rows = slice(place * TOK, (place + 1) * TOK)
        stats = []
        for h in range(HEADS):
            cols = slice(h * HD, (h + 1) * HD)
            scores = []
            for i in halves:
                s = dot(k[i * TOK : (i + 1) * TOK, cols], q[rows, cols], 1, 1) * factor
                if i == place and valid is not None:
                    s = jnp.where(valid, s, NEG)
                scores.append(s)
            m = jnp.max(functools.reduce(jnp.maximum, scores), axis=0, keepdims=True)
            probs = [jnp.exp2(s - m) for s in scores]
            total = jnp.sum(functools.reduce(jnp.add, probs), axis=0, keepdims=True)
            parts = [
                dot(v[cols, i * TOK : (i + 1) * TOK], p.astype(BF16), 1, 0)
                for i, p in zip(halves, probs)
            ]
            mix = functools.reduce(jnp.add, parts)
            out[cols, rows] = (mix * (1.0 / total)).astype(BF16)
            stats.append(m + jnp.log2(total))
        out[FEAT:, rows] = pack_stats(stats, TOK)

    for place in range(2):
        if distance == 1:
            half(place, (0, 1))
            continue
        later = (place + c) == 1
        both = later if distance == 0 else jnp.logical_not(later)
        pl.when(both)(functools.partial(half, place, (0, 1)))
        pl.when(jnp.logical_not(both))(functools.partial(half, place, (place,)))


def same_kernel(info, q, k, v, out):
    local_block(0, info, q, k, v, out)


def next_kernel(info, q1, q2, k, v, out):
    y, c = info[1], info[3]
    for near, here in ((q2, c == 0), (q1, c != 0)):

        @pl.when((y + 1 < RING) & here)
        def _():
            local_block(1, info, near, k, v, out)


def second_kernel(info, q3, k, v, _, out):
    @pl.when(info[1] + 2 < RING)
    def _():
        local_block(2, info, q3, k, v, out)


def held_specs(count):
    return [pl.BlockSpec(memory_space=pltpu.VMEM)] * count


def scalars(count):
    return [pl.BlockSpec(memory_space=pltpu.SMEM)] * count


def local_attention(kernel, info, queries, k, v, *earlier):
    count = 1
    slab = jax.ShapeDtypeStruct((SLAB, CHIP), BF16)
    return pl.pallas_call(
        kernel,
        in_specs=scalars(1) + held_specs(len(queries) + 2) + any_specs(len(earlier)),
        out_specs=held_specs(count),
        out_shape=[slab] * count,
        compiler_params=params(),
        cost_estimate=cost(4 * count * CHIP * CHIP * FEAT, 8 * CHIP * FEAT, 4 * CHIP * CHIP),
    )(info, *queries, k, v, *earlier)


def part_kernel(info, mem, out, flag, held, sem):
    start = pl.multiple_of(info[3] * FEAT, FEAT)
    src = mem.at[pl.ds(2 * info[1], 2), :, :, pl.ds(start, FEAT)]
    copy = pltpu.make_async_copy(src, held, sem)
    copy.start()
    copy.wait()
    for block in range(2):
        for h in range(HEADS):
            cols = slice(h * HD, (h + 1) * HD)
            out[0, h // GROUP, block, 0, h % GROUP] = held[block, 0, :, cols]
            out[0, h // GROUP, block, 1, h % GROUP] = held[block, 1, :, cols].T
    flag[...] = jnp.zeros_like(flag)


def take_part(info, memory):
    shape = (1, HEADS // GROUP, 2, 2, GROUP, BLK, HD)
    return pl.pallas_call(
        part_kernel,
        grid_spec=pltpu.PrefetchScalarGridSpec(
            num_scalar_prefetch=1,
            grid=(1,),
            in_specs=[pl.BlockSpec(memory_space=pltpu.HBM)],
            out_specs=[
                pl.BlockSpec(shape, lambda j, info: (0,) * 7),
                pl.BlockSpec((8, HD), lambda j, info: (0, 0)),
            ],
            scratch_shapes=[
                pltpu.VMEM((2, 2, BLK, FEAT), BF16),
                pltpu.SemaphoreType.DMA,
            ],
        ),
        out_shape=[
            jax.ShapeDtypeStruct(shape, BF16),
            jax.ShapeDtypeStruct((8, HD), F32),
        ],
        compiler_params=params(WIDE_VMEM),
        cost_estimate=cost(0, 2**20),
    )(info, memory)


def join_kernel(group, *refs):
    near, out, sem = refs[:RING], refs[-2], refs[-1]
    copies = [
        pltpu.make_async_copy(ref.at[:, group], out.at[pl.ds(s, 1)], sem.at[s])
        for s, ref in enumerate(near)
    ]
    for copy in copies:
        copy.start()
    for copy in copies:
        copy.wait()


def join(group, near, *earlier):
    shape = (RING, *near[0].shape[2:])
    return pl.pallas_call(
        functools.partial(join_kernel, group),
        in_specs=any_specs(len(near) + len(earlier)),
        out_specs=pl.BlockSpec(memory_space=pl.ANY),
        out_shape=jax.ShapeDtypeStruct(shape, BF16),
        scratch_shapes=[pltpu.SemaphoreType.DMA((RING,))],
        compiler_params=params(),
        cost_estimate=cost(0, 2**20),
    )(*near, *earlier)


def codes(info, ids):
    x, y, z, c = info[0], info[1], info[2], info[3]
    ax = (120 >> ((((ids >> 5) - x) & 3) * 2)) & 3
    az = (120 >> (((((ids >> 3) & 3) - z) & 3) * 2)) & 3
    slot = jnp.where(c == 0, az * 4 + ax, ax * 4 + az)
    mine = ((ids >> 1) & 3) == y
    return slot * 2 + (ids & 1) + 256 * mine.astype(jnp.int32)


def plan_kernel(info, ids, slots, blocks):
    def look(n, used):
        count = used
        for t in range(8):
            code = ids[n * 8 + t]
            slots[count] = code & 255
            blocks[count >> 1] = n
            count = count + (code >> 8)
        slots[count] = 32
        return count + (count & 1)

    used = lax.fori_loop(0, 16, look, 0)
    units = used >> 1
    for u in range(UNROLL - 1):
        blocks[units + u] = 16
        slots[used + 2 * u] = 0
        slots[used + 2 * u + 1] = 32
    blocks[79] = (units + UNROLL - 1) // UNROLL


def plan_units(info, ids):
    smem = pl.BlockSpec(memory_space=pltpu.SMEM)
    return pl.pallas_call(
        plan_kernel,
        in_specs=[smem] * 2,
        out_specs=[smem] * 2,
        out_shape=[
            jax.ShapeDtypeStruct((144,), jnp.int32),
            jax.ShapeDtypeStruct((80,), jnp.int32),
        ],
        compiler_params=params(),
        cost_estimate=cost(1000, 1000),
    )(info, ids)


def memory_kernel(group, slots, blocks, *refs):
    queries, parts, outs = refs[:4], refs[4:8], refs[8:12]
    q, mem, acc, top, low, o, sem, osem = refs[12:]
    wide = GROUP * HD
    copies = [
        pltpu.make_async_copy(ref, mem.at[pl.ds(4 * s, 4)], sem.at[4 + s])
        for s, ref in enumerate(parts)
    ]
    for s, ref in enumerate(queries):
        src = ref.at[pl.ds(0, CHIP), pl.ds(group * wide, wide)]
        copies.append(pltpu.make_async_copy(src, q.at[s], sem.at[s]))
    for copy in copies:
        copy.start()

    acc[...] = jnp.zeros_like(acc)
    top[...] = jnp.full_like(top, NEG)
    low[...] = jnp.zeros_like(low)
    for copy in copies:
        copy.wait()

    factor = HD ** -0.5 * LOG2E

    def pair(i, carry):
        work = []
        for u in [UNROLL * i + k for k in range(UNROLL)]:
            n = blocks[u]
            from_q = jnp.minimum(n, 15)
            start = pl.multiple_of((from_q & 3) * BLK, BLK)
            second = slots[2 * u + 1]
            work.append((n, from_q >> 2, start, slots[2 * u], second & 31, second < 32))
        scores = {}
        for j, (n, s, start, one, two, full) in enumerate(work):
            for h in range(GROUP):
                keys = jnp.concatenate([mem[one >> 1, one & 1, 0, h], mem[two >> 1, two & 1, 0, h]], axis=0)
                qh = q[s, pl.ds(start, BLK), h * HD : (h + 1) * HD]
                scores[j, h] = dot(keys, qh, 1, 1) * factor
        for j, (n, s, start, one, two, full) in enumerate(work):
            for h in range(GROUP):
                first, last = scores[j, h][:BLK], scores[j, h][BLK:]
                last = jnp.where(full, last, NEG)
                m_old = top[n, h]
                m = jnp.max(jnp.maximum(first, last), axis=0, keepdims=True)
                m = jnp.maximum(m_old, m)
                p = jnp.concatenate([jnp.exp2(first - m), jnp.exp2(last - m)], axis=0)
                alpha = jnp.exp2(m_old - m)
                top[n, h] = m
                low[n, h] = low[n, h] * alpha + jnp.sum(p, axis=0, keepdims=True)
                values = jnp.concatenate([mem[one >> 1, one & 1, 1, h], mem[two >> 1, two & 1, 1, h]], axis=1)
                acc[n, h] = acc[n, h] * alpha + dot(values, p.astype(BF16), 1, 0)
        return carry

    lax.fori_loop(0, blocks[79], pair, 0)

    backs = [
        pltpu.make_async_copy(o.at[s], ref, osem.at[s]) for s, ref in enumerate(outs)
    ]
    for s in (3, 1, 2, 0):
        for b in range(4):
            n = s * 4 + b
            cols = slice(b * BLK, (b + 1) * BLK)
            stats = []
            for h in range(GROUP):
                total = low[n, h]
                some = total > 0.0
                total = jnp.where(some, total, 1.0)
                o[s, h * HD : (h + 1) * HD, cols] = (acc[n, h] * (1.0 / total)).astype(BF16)
                stats.append(jnp.where(some, top[n, h] + jnp.log2(total), NEG))
            o[s, wide:, cols] = pack_stats(stats, BLK)
        backs[s].start()
    for copy in backs:
        copy.wait()


def memory_attention(group, plan, queries, parts):
    wide = GROUP * HD
    slab = jax.ShapeDtypeStruct((wide + STAT, CHIP), BF16)
    return pl.pallas_call(
        functools.partial(memory_kernel, group),
        grid_spec=pltpu.PrefetchScalarGridSpec(
            num_scalar_prefetch=2,
            grid=(1,),
            in_specs=any_specs(8),
            out_specs=any_specs(4),
            scratch_shapes=[
                pltpu.VMEM((4, CHIP, wide), BF16),
                pltpu.VMEM((16, 2, 2, GROUP, BLK, HD), BF16),
                pltpu.VMEM((17, GROUP, HD, BLK), F32),
                pltpu.VMEM((17, GROUP, 1, BLK), F32),
                pltpu.VMEM((17, GROUP, 1, BLK), F32),
                pltpu.VMEM((4, wide + STAT, CHIP), BF16),
                pltpu.SemaphoreType.DMA((8,)),
                pltpu.SemaphoreType.DMA((4,)),
            ],
        ),
        out_shape=[slab] * 4,
        compiler_params=params(),
        cost_estimate=cost(32 * 4 * BLK * BLK * wide, 24 * 1024 * wide, 32 * 4 * BLK * BLK),
    )(*plan, *queries, *parts)


def merge_kernel(info, gate, *refs):
    y = info[1]
    groups = HEADS // GROUP
    own, oth = refs[-2:]
    local = refs[4 * groups : 4 * groups + 3]

    def merged(refs, shown, h, stats, share):
        logs = []
        for ref, show in zip(refs, shown):
            rows = ref[stats:, :].astype(F32)
            log = rows[3 * h : 3 * h + 1] + rows[3 * h + 1 : 3 * h + 2]
            log = log + rows[3 * h + 2 : 3 * h + 3]
            logs.append(log if show is None else jnp.where(show, log, NEG))
        top = functools.reduce(jnp.maximum, logs)
        weights = [jnp.exp2(log - top) for log in logs]
        scale = share / functools.reduce(jnp.add, weights)
        total = None
        for ref, weight in zip(refs, weights):
            term = ref[h * HD : (h + 1) * HD, :].astype(F32) * (weight * scale)
            total = term if total is None else total + term
        return total

    for h in range(HEADS):
        g = jax.nn.sigmoid(jnp.full((1, CHIP), gate[info[3] * HEADS + h], F32))
        first = h // GROUP * 4
        mix = merged(refs[first : first + 4], (None,) * 4, h % GROUP, GROUP * HD, g)
        mix = mix + merged(local, (None, y >= 1, y >= 2), h, FEAT, 1.0 - g)
        mix = mix.astype(BF16)
        own[:, h * HD : (h + 1) * HD] = mix[:, :TOK].T
        oth[:, h * HD : (h + 1) * HD] = mix[:, TOK:].T


def merge(info, gate, slabs):
    return pl.pallas_call(
        merge_kernel,
        in_specs=scalars(2) + held_specs(len(slabs)),
        out_specs=held_specs(2),
        out_shape=[jax.ShapeDtypeStruct((TOK, FEAT), BF16)] * 2,
        compiler_params=params(),
        cost_estimate=cost(20 * SLAB * CHIP, 8 * 2 * SLAB * CHIP),
    )(info, gate, *slabs)


def output_kernel(info, own, oth, w, out):
    c = info[3]
    mine = pl.ds(pl.multiple_of(c * FEAT, FEAT), FEAT)
    other = pl.ds(pl.multiple_of((1 - c) * FEAT, FEAT), FEAT)
    tile = 512
    for j in range(out.shape[1] // tile):
        cols = slice(j * tile, (j + 1) * tile)
        total = dot(own[...], w[mine, cols], 1, 0) + dot(oth[...], w[other, cols], 1, 0)
        out[:, cols] = total.astype(BF16)


def project_output(info, own, oth, w):
    def whole(array):
        return pl.BlockSpec(array.shape, lambda j, info: (0, 0))

    result = jax.ShapeDtypeStruct((TOK, w.shape[1]), BF16)
    return pl.pallas_call(
        output_kernel,
        grid_spec=pltpu.PrefetchScalarGridSpec(
            num_scalar_prefetch=1,
            grid=(1,),
            in_specs=[whole(own), whole(oth), whole(w)],
            out_specs=whole(result),
        ),
        out_shape=result,
        compiler_params=params(),
        cost_estimate=cost(4 * TOK * FEAT * w.shape[1], 4 * FEAT * w.shape[1]),
    )(info, own, oth, w)


def shards(tokens, block_ids, memory, w_query, w_key, w_value, w_out, gate_bias):
    mem = lax.axis_index("mem")
    seq = lax.axis_index("seq")
    y, c = seq // 2, seq % 2
    info = jnp.stack([mem // RING, y, mem % RING, c]).astype(jnp.int32)

    own = tokens[0]
    oth = send(own, core)
    ids_own = block_ids.reshape(1, 16)
    ids_chip = jnp.concatenate([ids_own, send(ids_own, core)], axis=1)
    ids_rows = jnp.zeros((STAT, FEAT), BF16).at[0:1, 0:32].set(ids_chip.astype(BF16))

    groups = HEADS // GROUP
    part, taken = take_part(info, memory)
    near = [part] + [send(part, gather_move(0, d)) for d in (1, -1, 2)]

    query = project_query(info, own, oth, w_query, ids_rows, taken)
    query1 = send(query, around(1))
    query2 = send(query, around(-1))
    k, v = project_keyvalue(info, own, oth, w_key, w_value, query)
    query3 = send(query1, around(1))
    queries = [query, query1, query2, query3]

    parts = []
    for g in range(groups):
        mine = join(g, near, *((query1, k) if g == 1 else ()))
        below = send(mine, gather_move(1, 1))
        above = send(mine, gather_move(1, -1))
        far = send(below, gather_move(1, 1)) if g % 2 == 0 else send(above, gather_move(1, -1))
        parts.append((mine, below, above, far))

    (local0,) = local_attention(same_kernel, info, [query], k, v)
    ids = jnp.concatenate([q[CHIP, 0:32] for q in queries]).astype(jnp.int32)
    plan = plan_units(info, codes(info, ids))
    (local1,) = local_attention(next_kernel, info, queries[1:3], k, v)
    (local2,) = local_attention(second_kernel, info, queries[3:], k, v, local1)
    local1 = send(local1, later1)
    local2 = send(local2, later2)

    slabs = []
    for g in range(groups):
        mine, one, two, far = memory_attention(g, plan, queries, parts[g])
        slabs += [mine, send(one, around(-1)), send(two, around(1)), send(far, around(2))]
    mix_own, mix_oth = merge(info, gate_bias, slabs + [local0, local1, local2])
    mix_oth = send(mix_oth, core)
    return project_output(info, mix_own, mix_oth, w_out)[None]


def solution(mesh):
    in_specs = (
        P("mem", "seq", None),
        P("mem", "seq", None),
        P("mem", None, None, None),
        P(),
        P(),
        P(),
        P(),
        P(),
    )
    out_specs = P("mem", "seq", None)
    return jax.shard_map(shards, mesh=mesh, in_specs=in_specs, out_specs=out_specs, check_vma=False)
```
